256 devices in a mesh: lat: 8 (over y, x_hi), lon: 32 (over z, x_lo, core).
Axes of the slice: x: 4 (x_hi: 2, x_lo: 2; x = x_hi * 2 + x_lo), y: 4, z: 8, core: 2. Of those that a mesh axis runs over, the one named last changes fastest.
Arguments:
- checkpoint: float32 [4, 8, 256, 2048], P(None, None, 'lon', 'lat'), may hold values from -6 to 6
- courant_lon: float32 [8, 256, 2048], P(None, 'lon', 'lat'), may hold values from -0.6 to 0.6
- courant_lat: float32 [8, 256, 2048], P(None, 'lon', 'lat'), may hold values from -0.6 to 0.6
- mixing: float32 [8, 256, 2048], P(None, 'lon', 'lat'), may hold values from 0.05 to 5
- limiter_flags: int32 [4, 4, 8, 256, 2048], P(None, None, None, 'lon', 'lat'), may hold values from 0 to 8
- column_weights: float32 [8], replicated, may hold values from 0.1 to 1
- observations: float32 [4, 4, 256, 2048], P(None, None, 'lon', 'lat'), may hold values from -12 to 12
- misfit_weight: float32 [4, 256, 2048], P(None, 'lon', 'lat'), may hold values from 0.2 to 2
Outputs:
- final_state: float32 [4, 8, 256, 2048], P(None, None, 'lon', 'lat')
- gradient: float32 [4, 8, 256, 2048], P(None, None, 'lon', 'lat')
The draws below stay inside these ranges and needn't reach their ends.
Inputs may be any that keep to these rules, and one draw needn't show every extreme that they name: `limiter_flags`: each value holds the longitude branch as its remainder by 3 and the latitude branch as its quotient by 3.
All inputs are finite; a program needn't handle non-finite values.
Results may differ from the reference program's by a relative error of at most 0.0003.
Values sent between devices are 32-bit elements; how exact they have to be, the bound alone decides.
No kernel may reach another device: no remote copies, remote signals or barrier semaphores. Data moves between devices by JAX's collectives and lax.ppermute only.
A program may use at most 64 MiB of HBM per device.

```python
import math
import jax
import jax.numpy as jnp
from jax import lax

TRACERS = 4
LEVELS = 8
SUBSTEPS = 4
NLON = 256
NLAT = 2048


def with_ends(values, rng, smallest, largest):
    place = [jax.random.randint(jax.random.fold_in(rng, axis), (), 0, length) for axis, length in enumerate(values.shape)]
    longest = values.shape.index(max(values.shape))
    neighbour = place[:longest] + [(place[longest] + 1) % values.shape[longest]] + place[longest + 1:]
    return values.at[tuple(place)].set(smallest).at[tuple(neighbour)].set(largest)


def block_scale(own_key, shape, shards, low, largest):
    level, own = 1.0, jax.random.fold_in(own_key, 6)
    for dim, blocks in shards:
        heights = jnp.exp(jax.random.uniform(jax.random.fold_in(own, dim), (blocks,), jnp.float32, low / len(shards), largest / len(shards)))
        level = level * jnp.repeat(heights, shape[dim] // blocks).reshape([-1 if axis == dim else 1 for axis in range(len(shape))])
    return level


def noise(stream_key, dims, scale, most, cuts=(), kind=jnp.bfloat16):
    entries = scale * jax.random.normal(stream_key, dims, jnp.float32)
    if cuts:
        entries = entries * block_scale(stream_key, dims, cuts, -0.22, 0.18)
    return jnp.clip(entries, -most, most).astype(kind)


def setup_inputs(seed: int = 0) -> dict:
    streams_of = jax.random.split(jax.random.key(seed), 9)
    checkpoint = noise(streams_of[0], (TRACERS, LEVELS, NLON, NLAT), 1.0, 6.0, ((2, 32), (3, 8)), jnp.float32)
    courant_lon = jnp.clip(jax.random.uniform(streams_of[1], (LEVELS, NLON, NLAT), jnp.float32, -0.6, 0.6) * block_scale(streams_of[1], (LEVELS, NLON, NLAT), ((1, 32), (2, 8)), -0.4, 0.0), -0.6, 0.6)
    courant_lat = jnp.clip(jax.random.uniform(streams_of[2], (LEVELS, NLON, NLAT), jnp.float32, -0.6, 0.6) * block_scale(streams_of[2], (LEVELS, NLON, NLAT), ((1, 32), (2, 8)), -0.4, 0.0), -0.6, 0.6)
    mixing = jnp.clip(jnp.exp(math.log(5.0) - 4.6051702 * jax.random.uniform(streams_of[3], (LEVELS, NLON, NLAT), jnp.float32) ** block_scale(streams_of[3], (LEVELS, NLON, NLAT), ((1, 32), (2, 8)), -0.2, 0.2)), 0.05, 5.0)
    limiter_flags = with_ends(jax.random.randint(streams_of[4], (SUBSTEPS, TRACERS, LEVELS, NLON, NLAT), 0, 9), jax.random.fold_in(streams_of[4], 1), 0, 8).astype(jnp.int32)
    column_weights = jnp.clip(jnp.exp(jax.random.uniform(streams_of[5], (LEVELS,), jnp.float32, math.log(0.1), math.log(1.0))), 0.1, 1.0)
    observations = noise(streams_of[6], (SUBSTEPS, TRACERS, NLON, NLAT), 2.0, 12.0, ((2, 32), (3, 8)), jnp.float32)
    misfit_weight = jnp.clip(jnp.exp(math.log(2.0) - 2.3025851 * jax.random.uniform(streams_of[7], (TRACERS, NLON, NLAT), jnp.float32) ** block_scale(streams_of[7], (TRACERS, NLON, NLAT), ((1, 32), (2, 8)), -0.2, 0.2)), 0.2, 2.0)
    return dict(checkpoint=checkpoint, courant_lon=courant_lon, courant_lat=courant_lat, mixing=mixing, limiter_flags=limiter_flags, column_weights=column_weights, observations=observations, misfit_weight=misfit_weight)


def face_flux(behind, current, next_cell, beyond, courant, branches):
    forward = courant >= 0.0
    upwind = jnp.where(forward, current, next_cell)
    downwind = jnp.where(forward, next_cell, current)
    farther = jnp.where(forward, behind, beyond)
    increment = jnp.where(branches == 1, downwind - upwind, jnp.where(branches == 2, upwind - farther, jnp.zeros_like(upwind)))
    return courant * (upwind + 0.5 * (1.0 - jnp.abs(courant)) * increment)

def flux_sweep(padded, courant, branches, along):
    length = padded.shape[along] - 4

    def section(source, first, extent):
        return lax.slice_in_dim(source, first, first + extent, axis=along)
    flux = face_flux(section(padded, 0, length + 1), section(padded, 1, length + 1), section(padded, 2, length + 1), section(padded, 3, length + 1), courant, branches)
    return section(padded, 2, length) - (section(flux, 1, length) - section(flux, 0, length))

def factor(mixing):
    levels = mixing.shape[0]
    below_top = (jnp.arange(levels) < levels - 1).astype(mixing.dtype)
    coupling = mixing * below_top.reshape((levels,) + (1,) * (mixing.ndim - 1))
    ratios = []
    inverses = []
    for level_index in range(levels):
        pivot = 1.0 + coupling[level_index]
        if level_index > 0:
            pivot = pivot + coupling[level_index - 1] - coupling[level_index - 1] * ratios[-1]
        inverse = 1.0 / pivot
        inverses.append(inverse)
        ratios.append(coupling[level_index] * inverse)
    return (coupling, jnp.stack(ratios), jnp.stack(inverses))

def vertical_solve(values, coupling, ratios, inverses):
    levels = values.shape[0]
    forward_rows = []
    for level_index in range(levels):
        running = values[level_index]
        if level_index > 0:
            running = running + coupling[level_index - 1] * forward_rows[-1]
        forward_rows.append(running * inverses[level_index])
    results = [forward_rows[-1]]
    for level_index in range(levels - 2, -1, -1):
        results.append(forward_rows[level_index] + ratios[level_index] * results[-1])
    return jnp.stack(results[::-1])

def reference(checkpoint, courant_lon, courant_lat, mixing, limiter_flags, column_weights, observations, misfit_weight):
    lat_count = courant_lat.shape[-1]
    substeps = observations.shape[0]
    pole_mask = (jnp.arange(lat_count) < lat_count - 1).astype(courant_lat.dtype)
    north_faces = courant_lat * pole_mask
    lat_branch = limiter_flags // 3
    lon_branch = limiter_flags - 3 * lat_branch
    coupling, ratios, inverses = factor(mixing)
    lon_courant = jnp.concatenate([courant_lon[:, -1:], courant_lon], axis=1)
    lat_courant = jnp.pad(north_faces, ((0, 0), (0, 0), (1, 0)))
    level_weights = column_weights.reshape((-1, 1, 1))

    def per_tracer(inputs):
        start, branches_lon, branches_lat, targets, weights = inputs
        lon_flags = jnp.concatenate([branches_lon[:, :, -1:], branches_lon], axis=2)
        lat_flags = jnp.pad(branches_lat, ((0, 0), (0, 0), (0, 0), (1, 0)))

        def advance(values, substep):
            wrapped = jnp.concatenate([values[:, -2:], values, values[:, :2]], axis=1)
            values = flux_sweep(wrapped, lon_courant, lon_flags[substep], 1)
            padded = jnp.pad(values, ((0, 0), (0, 0), (2, 2)))
            values = flux_sweep(padded, lat_courant, lat_flags[substep], 2)
            return vertical_solve(values, coupling, ratios, inverses)

        def forcing(values, substep):
            misfit = lax.optimization_barrier(jnp.sum(level_weights * values, axis=0)) - targets[substep]
            return level_weights * (weights * misfit)[None]
        history = [start]
        for substep in range(substeps):
            history.append(advance(history[-1], substep))
        adjoint = forcing(history[substeps], substeps - 1)
        for substep in range(substeps, 0, -1):
            adjoint = jax.vjp(lambda source: advance(source, substep - 1), history[substep - 1])[1](adjoint)[0]
            if substep > 1:
                adjoint = adjoint + forcing(history[substep - 1], substep - 2)
        return (history[substeps], adjoint)
    final_state, gradient = lax.map(per_tracer, (checkpoint, jnp.moveaxis(lon_branch, 1, 0), jnp.moveaxis(lat_branch, 1, 0), jnp.moveaxis(observations, 1, 0), misfit_weight))
    return (final_state, gradient)
```

```python
import jax
import jax.numpy as jnp
from jax import lax
from jax.experimental import pallas as pl
from jax.experimental.pallas import tpu as pltpu
from jax.sharding import PartitionSpec as P

TRACERS, LEVELS, SUBSTEPS = 4, 8, 4
COLS, ROWS, EDGE, LANES = 8, 256, 16, 128
WIDE = ROWS + LANES
STATE = TRACERS * LEVELS
LIMIT = 50 * 1024 * 1024
CORNER = 23


def lane_ids():
    return lax.broadcasted_iota(jnp.int32, (COLS, LANES), 1)


def col_ids(lanes=LANES):
    return lax.broadcasted_iota(jnp.int32, (COLS, lanes), 0)


def pack(ck, cl, ct, mx, fl, obs, mw, to_right, to_left, to_north, to_south):
    lane, col = (lane_ids(), col_ids(ROWS))
    to_right[0:STATE] = ck[...]
    to_left[0:STATE] = ck[...]
    for place, field in ((32, cl), (40, ct), (48, mx)):
        to_right[place : place + LEVELS] = field[...]
        to_left[place : place + LEVELS] = field[...]

    def flags(substep, row):
        return fl[substep * STATE + row].astype(jnp.float32)

    @pl.loop(0, TRACERS)
    def _(tracer):
        for level in range(LEVELS):
            row = tracer * LEVELS + level
            one, two, three, four = [flags(s, row) for s in range(SUBSTEPS)]
            to_right[56 + row] = jnp.where(col >= 1, one, pltpu.roll(four, 1, 0))
            to_right[88 + row] = jnp.where(col >= 3, two, pltpu.roll(three, 3, 0))
            to_left[56 + row] = jnp.where(col < 6, one, pltpu.roll(three, 6, 0))
            if level < 4:
                other = flags(1, row + 4)
                to_left[88 + tracer * 4 + level] = jnp.where(col < 4, two, pltpu.roll(other, 4, 0))

    def strips(place, read, count):
        north = jnp.zeros((COLS, LANES), jnp.float32)
        south = north
        for k in range(count):
            here = (lane >= EDGE * k) & (lane < EDGE * (k + 1))
            whole = read(k)
            north = jnp.where(here, pltpu.roll(whole[:, LANES:], (EDGE * (k + 1)) % LANES, 1), north)
            south = jnp.where(here, pltpu.roll(whole[:, :LANES], EDGE * k, 1), south)
        to_north[place] = north
        to_south[place] = south

    @pl.loop(0, TRACERS)
    def _(tracer):
        strips(tracer, lambda k: ck[tracer * LEVELS + k], LEVELS)

    for place, field in ((4, cl), (5, ct), (6, mx)):
        strips(place, lambda k, field=field: field[k], LEVELS)

    @pl.loop(0, SUBSTEPS * TRACERS)
    def _(block):
        strips(7 + block, lambda k: fl[block * LEVELS + k].astype(jnp.float32), LEVELS)

    for half in range(2):
        strips(23 + half, lambda k, half=half: obs[half * 8 + k], 8)
    strips(25, lambda k: mw[k], TRACERS)


def behind(value, axis):
    return pltpu.roll(value, 1, axis)


def ahead(value, axis):
    return pltpu.roll(value, value.shape[axis] - 1, axis)


def weights(branch, low, high, c_minus, c_both, slope):
    first = jnp.where(branch >= high, c_minus, jnp.where(branch >= low, c_both, c_minus))
    return first, jnp.where(branch >= high, slope, 0.0)


def sweep(value, courant, first, second, axis):
    step = ahead(value, axis) - value
    farther = jnp.where(courant >= 0.0, behind(step, axis), ahead(step, axis))
    flux = courant * value + first * step + second * farther
    return value - flux + behind(flux, axis)


def sweep_back(value, courant, first, second, axis):
    step = ahead(value, axis) - value
    reach = second * step
    forward = jnp.where(courant >= 0.0, reach, 0.0)
    total = first * step + ahead(forward, axis) + behind(reach - forward, axis)
    return value + courant * step + behind(total, axis) - total


def slopes(courant):
    c_minus = jnp.minimum(courant, 0.0)
    size = jnp.abs(courant)
    slope = 0.5 * size * (1.0 - size)
    return c_minus, c_minus + slope, slope


def window(
    ck, cl, ct, mx, fl, obs, mw, cw, from_left, from_right, north, south, left_corner, right_corner,
    final, grad, grad_left, grad_right,
    q, temp, lon_code, lat_code, cx, cy, cy_minus, cy_both, cy_slope, inv, elim, ratio, obs_w, mw_w, force,
):
    lane, col = (lane_ids(), col_ids())
    col_w = col_ids(WIDE)

    def tail(n_tile, s_tile, k):
        n_part = pltpu.roll(n_tile, (LANES - EDGE * k) % LANES, 1)
        s_part = pltpu.roll(s_tile, (LANES - EDGE - EDGE * k) % LANES, 1)
        return jnp.where(lane < EDGE, n_part, jnp.where(lane >= LANES - EDGE, s_part, 0.0))

    def own_tail(place, k):
        return tail(north[place], south[place], k)

    def left_tail(place, k):
        return tail(left_corner[place], left_corner[CORNER + place], k)

    def right_tail(place, k):
        return tail(right_corner[place], right_corner[CORNER + place], k)

    def wide(main, end):
        return jnp.concatenate([main, end], axis=1)

    def squeeze(right, left):
        return jnp.where(col_w < 4, right, left)

    @pl.loop(0, TRACERS)
    def _(tracer):
        for level in range(LEVELS):
            row = tracer * LEVELS + level
            q[row, 0] = wide(ck[row], own_tail(tracer, level))
            q[row, 1] = wide(from_right[row], right_tail(tracer, level))
            q[row, 2] = wide(from_left[row], left_tail(tracer, level))

    lane_w = lax.broadcasted_iota(jnp.int32, (COLS, WIDE), 1)
    last = lax.axis_index("lat") == lax.axis_size("lat") - 1
    pole = (lane_w == ROWS - 1) & last
    carry = [None] * 4
    for level in range(LEVELS):
        def blocks(field, place):
            at = 32 + 8 * (place - 4) + level
            own = wide(field[level], own_tail(place, level))
            right = wide(from_right[at], right_tail(place, level))
            left = wide(from_left[at], left_tail(place, level))
            return [own, right, left, squeeze(right, left)]

        for k, value in enumerate(blocks(cl, 4)):
            cx[level, k] = value
        for k, value in enumerate(blocks(ct, 5)):
            value = jnp.where(pole, 0.0, value)
            c_minus, c_both, slope = slopes(value)
            cy[level, k] = value
            cy_minus[level, k] = c_minus
            cy_both[level, k] = c_both
            cy_slope[level, k] = slope
        for k, value in enumerate(blocks(mx, 6)):
            coupling = value if level < LEVELS - 1 else jnp.zeros_like(value)
            pivot = 1.0 + coupling
            if level > 0:
                above, above_ratio = carry[k]
                pivot = pivot + above - above * above_ratio
            inverse = 1.0 / pivot
            inv[level, k] = inverse
            ratio[level, k] = coupling * inverse
            elim[level, k] = above * inverse if level > 0 else jnp.zeros_like(value)
            carry[k] = (coupling, coupling * inverse)

    for k in range(SUBSTEPS * TRACERS):
        obs_w[k] = wide(obs[k], own_tail(23 + k // 8, k % 8))
    for k in range(TRACERS):
        mw_w[k] = wide(mw[k], own_tail(25, k))

    def put_codes(substep, row, blocks, lat_blocks):
        for k, value in enumerate(blocks):
            lon_code[substep, row, k] = value - jnp.where(value >= 6.0, 6.0, jnp.where(value >= 3.0, 3.0, 0.0))
        for k, value in enumerate(lat_blocks):
            lat_code[substep, row, k] = value

    @pl.loop(0, TRACERS)
    def _(tracer):
        for level in range(LEVELS):
            row = tracer * LEVELS + level
            own = [
                wide(fl[s * STATE + row].astype(jnp.float32), own_tail(7 + s * TRACERS + tracer, level))
                for s in range(SUBSTEPS)
            ]
            r_tail = [right_tail(7 + s * TRACERS + tracer, level) for s in range(3)]
            l_tail = [left_tail(7 + s * TRACERS + tracer, level) for s in range(SUBSTEPS)]
            l_a, l_b = (from_left[56 + row], from_left[88 + row])
            r_a = from_right[56 + row]
            r_b = from_right[88 + tracer * 4 + level % 4]
            if level >= 4:
                r_b = pltpu.roll(r_b, 4, 0)
            one = [own[0], wide(r_a, r_tail[0]), wide(l_a, l_tail[0])]
            put_codes(0, row, one, one)
            two = [own[1], wide(r_b, r_tail[1]), wide(l_b, l_tail[1])]
            put_codes(1, row, two, [own[1], squeeze(two[1], two[2])])
            three = [
                own[2],
                squeeze(wide(pltpu.roll(r_a, 2, 0), r_tail[2]), wide(pltpu.roll(l_b, 5, 0), l_tail[2])),
            ]
            put_codes(2, row, three, three)
            four = [own[3], wide(pltpu.roll(l_a, 7, 0), l_tail[3])]
            put_codes(3, row, four, [own[3]])

    def lon_pass(substep, source, target, slots, back, chunks=3):
        code_slots = slots if len(slots) == 3 else (0, 1)

        @pl.loop(0, LEVELS)
        def _(level):
            for chunk in range(chunks):
                at = slice(chunk * LANES, (chunk + 1) * LANES)
                c = jnp.concatenate([cx[level, k, :, at] for k in slots], axis=0)
                c_minus, c_both, slope = slopes(c)
                for tracer in range(TRACERS):
                    row = tracer * LEVELS + level
                    value = jnp.concatenate([source[row, k, :, at] for k in slots], axis=0)
                    code = jnp.concatenate([lon_code[substep, row, k, :, at] for k in code_slots], axis=0)
                    first, second = weights(code, 1.0, 2.0, c_minus, c_both, slope)
                    out = (sweep_back if back else sweep)(value, c, first, second, 0)
                    for n, k in enumerate(slots):
                        target(row, k, at, out[n * COLS : (n + 1) * COLS])

    def to_temp(row, k, at, value):
        temp[row, k, :, at] = value

    def to_q(row, k, at, value):
        q[row, k, :, at] = value

    def to_grad(row, k, at, value):
        (grad, grad_right, grad_left)[k][row, :, at] = value

    def lat_weights(substep, row, level, code_slot, slot):
        return weights(
            lat_code[substep, row, code_slot], 3.0, 6.0, cy_minus[level, slot], cy_both[level, slot], cy_slope[level, slot]
        )

    def solve(read, slot):
        forward = []
        for level in range(LEVELS):
            running = read(level) * inv[level, slot]
            if level > 0:
                running = running + elim[level, slot] * forward[-1]
            forward.append(running)
        results = [forward[-1]]
        for level in range(LEVELS - 2, -1, -1):
            results.append(forward[level] + ratio[level, slot] * results[-1])
        return results[::-1]

    def lat_and_mix(substep, slots):
        @pl.loop(0, TRACERS)
        def _(tracer):
            for slot in slots:
                code_slot = 1 if slot == 3 else slot

                def read(level):
                    row = tracer * LEVELS + level
                    if slot == 3 and substep == 1:
                        value = squeeze(temp[row, 1], temp[row, 2])
                    else:
                        value = temp[row, slot]
                    first, second = lat_weights(substep, row, level, code_slot, slot)
                    return sweep(value, cy[level, slot], first, second, 1)

                results = solve(read, slot)
                if slot == 0:
                    column = cw[0] * results[0]
                    for level in range(1, LEVELS):
                        column = column + cw[level] * results[level]
                    at = substep * TRACERS + tracer
                    force[at] = mw_w[tracer] * (column - obs_w[at])
                for level in range(LEVELS):
                    row = tracer * LEVELS + level
                    if substep == SUBSTEPS - 1:
                        final[row] = results[level][:, :ROWS]
                    else:
                        q[row, slot] = results[level]

    def mix_and_lat(substep, slots):
        @pl.loop(0, TRACERS)
        def _(tracer):
            for slot in slots:
                code_slot = 1 if slot == 3 else slot

                def read(level):
                    row = tracer * LEVELS + level
                    if slot != 0:
                        return q[row, slot]
                    added = cw[level] * force[substep * TRACERS + tracer]
                    return added if substep == SUBSTEPS - 1 else q[row, slot] + added

                results = solve(read, slot)
                for level in range(LEVELS):
                    row = tracer * LEVELS + level
                    first, second = lat_weights(substep, row, level, code_slot, slot)
                    out = sweep_back(results[level], cy[level, slot], first, second, 1)
                    if slot == 3 and substep == 1:
                        temp[row, 1] = jnp.where(col_w < 4, out, 0.0)
                        temp[row, 2] = jnp.where(col_w < 4, 0.0, out)
                    else:
                        temp[row, slot] = out
                    if substep == SUBSTEPS - 1:
                        temp[row, 3] = jnp.zeros_like(out)

    three, two = ((0, 1, 2), (0, 3))
    lon_pass(0, q, to_temp, three, False)
    lat_and_mix(0, three)
    lon_pass(1, q, to_temp, three, False)
    lat_and_mix(1, two)
    lon_pass(2, q, to_temp, two, False)
    lat_and_mix(2, two)
    lon_pass(3, q, to_temp, two, False)
    lat_and_mix(3, (0,))
    mix_and_lat(3, (0,))
    lon_pass(3, temp, to_q, two, True)
    mix_and_lat(2, two)
    lon_pass(2, temp, to_q, two, True)
    mix_and_lat(1, two)
    lon_pass(1, temp, to_q, three, True)
    mix_and_lat(0, three)
    lon_pass(0, temp, to_grad, three, True, 2)


def whole_spec(count):
    return [pl.BlockSpec(memory_space=pltpu.VMEM)] * count


def shards(
    checkpoint, courant_lon, courant_lat, mixing, limiter_flags, column_weights, observations, misfit_weight
):
    f32 = jnp.float32
    lat, lon = (lax.axis_size("lat"), lax.axis_size("lon"))
    east = [(i, (i + 1) % lon) for i in range(lon)]
    west = [(j, i) for i, j in east]
    up = [(i, i + 1) for i in range(lat - 1)]
    down = [(j, i) for i, j in up]
    own = (
        checkpoint.reshape((STATE, COLS, ROWS)),
        courant_lon,
        courant_lat,
        mixing,
        limiter_flags.reshape((SUBSTEPS * STATE, COLS, ROWS)),
        observations.reshape((SUBSTEPS * TRACERS, COLS, ROWS)),
        misfit_weight,
    )
    params = pltpu.CompilerParams(vmem_limit_bytes=LIMIT)
    to_right, to_left, to_north, to_south = pl.pallas_call(
        pack,
        out_shape=(
            jax.ShapeDtypeStruct((120, COLS, ROWS), f32),
            jax.ShapeDtypeStruct((104, COLS, ROWS), f32),
            jax.ShapeDtypeStruct((26, COLS, LANES), f32),
            jax.ShapeDtypeStruct((26, COLS, LANES), f32),
        ),
        in_specs=whole_spec(7),
        out_specs=tuple(whole_spec(4)),
        compiler_params=params,
        name="pack",
    )(*own)
    from_left = lax.ppermute(to_right, "lon", east)
    from_right = lax.ppermute(to_left, "lon", west)
    south = lax.ppermute(to_north, "lat", up)
    north = lax.ppermute(to_south, "lat", down)
    corner = jnp.concatenate([north[:CORNER], south[:CORNER]], axis=0)
    left_corner = lax.ppermute(corner, "lon", east)
    right_corner = lax.ppermute(corner, "lon", west)
    small = pltpu.VMEM((LEVELS, 4, COLS, WIDE), f32)
    block = jax.ShapeDtypeStruct((STATE, COLS, ROWS), f32)
    final, grad, grad_left, grad_right = pl.pallas_call(
        window,
        out_shape=(block,) * 4,
        in_specs=whole_spec(7) + [pl.BlockSpec(memory_space=pltpu.SMEM)] + whole_spec(6),
        out_specs=tuple(whole_spec(4)),
        scratch_shapes=[
            pltpu.VMEM((STATE, 4, COLS, WIDE), f32),
            pltpu.VMEM((STATE, 4, COLS, WIDE), f32),
            pltpu.VMEM((SUBSTEPS, STATE, 3, COLS, WIDE), f32),
            pltpu.VMEM((SUBSTEPS, STATE, 3, COLS, WIDE), f32),
        ]
        + [small] * 8
        + [
            pltpu.VMEM((SUBSTEPS * TRACERS, COLS, WIDE), f32),
            pltpu.VMEM((TRACERS, COLS, WIDE), f32),
            pltpu.VMEM((SUBSTEPS * TRACERS, COLS, WIDE), f32),
        ],
        compiler_params=params,
        name="window",
    )(*own, column_weights, from_left, from_right, north, south, left_corner, right_corner)
    grad = grad + lax.ppermute(grad_left, "lon", west) + lax.ppermute(grad_right, "lon", east)
    return (final.reshape(checkpoint.shape), grad.reshape(checkpoint.shape))


def solution(mesh):
    return jax.shard_map(
        shards,
        mesh=mesh,
        in_specs=(
            P(None, None, "lon", "lat"),
            P(None, "lon", "lat"),
            P(None, "lon", "lat"),
            P(None, "lon", "lat"),
            P(None, None, None, "lon", "lat"),
            P(),
            P(None, None, "lon", "lat"),
            P(None, "lon", "lat"),
        ),
        out_specs=(P(None, None, "lon", "lat"), P(None, None, "lon", "lat")),
        check_vma=False,
    )
```

```python
import jax
import jax.numpy as jnp
from jax import lax
from jax.experimental import pallas as pl
from jax.experimental.pallas import tpu as pltpu
from jax.sharding import PartitionSpec as P

TRACERS, LEVELS, SUBSTEPS = 4, 8, 4
PAIR = 2
COLS, ROWS, EDGE, LANES = 8, 256, 16, 128
STATE = TRACERS * LEVELS
HALF = PAIR * LEVELS
LIMIT = 40 * 1024 * 1024
CORNER = 23


def lane_ids():
    return lax.broadcasted_iota(jnp.int32, (COLS, LANES), 1)


def col_ids(lanes=LANES):
    return lax.broadcasted_iota(jnp.int32, (COLS, lanes), 0)


def pack(*refs):
    hbm, (right_a, right_b, left_a, left_b, to_north, to_south), own, sems = (refs[:7], refs[7:13], refs[13:20], refs[20])
    copies = [pltpu.make_async_copy(hbm[k], own[k], sems.at[k]) for k in range(7)]
    for copy in copies:
        copy.start()
    for copy in copies:
        copy.wait()
    ck, cl, ct, mx, fl, obs, mw = own
    lane, col = (lane_ids(), col_ids(ROWS))
    for half, (to_right, to_left) in enumerate(((right_a, left_a), (right_b, left_b))):
        to_right[0:HALF] = ck[half * HALF : (half + 1) * HALF]
        to_left[0:HALF] = ck[half * HALF : (half + 1) * HALF]

        @pl.loop(0, PAIR)
        def _(tracer):
            for level in range(LEVELS):
                row = tracer * LEVELS + level
                one, two, three, four = [
                    fl[s * STATE + half * HALF + row].astype(jnp.float32) for s in range(SUBSTEPS)
                ]
                to_right[HALF + row] = jnp.where(col >= 1, one, pltpu.roll(four, 1, 0))
                to_right[2 * HALF + row] = jnp.where(col >= 3, two, pltpu.roll(three, 3, 0))
                to_left[HALF + row] = jnp.where(col < 6, one, pltpu.roll(three, 6, 0))
                if level < 4:
                    other = fl[STATE + half * HALF + row + 4].astype(jnp.float32)
                    to_left[2 * HALF + tracer * 4 + level] = jnp.where(col < 4, two, pltpu.roll(other, 4, 0))

    for k, field in enumerate((cl, ct, mx)):
        right_a[3 * HALF + 8 * k : 3 * HALF + 8 * k + 8] = field[...]
        left_a[40 + 8 * k : 48 + 8 * k] = field[...]

    def strips(place, read, count):
        north = jnp.zeros((COLS, LANES), jnp.float32)
        south = north
        for k in range(count):
            here = (lane >= EDGE * k) & (lane < EDGE * (k + 1))
            whole = read(k)
            north = jnp.where(here, pltpu.roll(whole[:, LANES:], (EDGE * (k + 1)) % LANES, 1), north)
            south = jnp.where(here, pltpu.roll(whole[:, :LANES], EDGE * k, 1), south)
        to_north[place] = north
        to_south[place] = south

    @pl.loop(0, TRACERS)
    def _(tracer):
        strips(tracer, lambda k: ck[tracer * LEVELS + k], LEVELS)

    for place, field in ((4, cl), (5, ct), (6, mx)):
        strips(place, lambda k, field=field: field[k], LEVELS)

    @pl.loop(0, SUBSTEPS * TRACERS)
    def _(block):
        strips(7 + block, lambda k: fl[block * LEVELS + k].astype(jnp.float32), LEVELS)

    for half in range(2):
        strips(23 + half, lambda k, half=half: obs[half * 8 + k], 8)
    strips(25, lambda k: mw[k], TRACERS)


def behind(value, axis):
    return pltpu.roll(value, 1, axis)


def ahead(value, axis):
    return pltpu.roll(value, value.shape[axis] - 1, axis)


def weights(branch, low, high, c_minus, c_both, slope):
    first = jnp.where(branch >= high, c_minus, jnp.where(branch >= low, c_both, c_minus))
    return first, jnp.where(branch >= high, slope, 0.0)


def sweep(value, courant, first, second, axis):
    step = ahead(value, axis) - value
    farther = jnp.where(courant >= 0.0, behind(step, axis), ahead(step, axis))
    flux = courant * value + first * step + second * farther
    return value - flux + behind(flux, axis)


def sweep_back(value, courant, first, second, axis):
    step = ahead(value, axis) - value
    reach = second * step
    forward = jnp.where(courant >= 0.0, reach, 0.0)
    total = first * step + ahead(forward, axis) + behind(reach - forward, axis)
    return value + courant * step + behind(total, axis) - total


def slopes(courant):
    c_minus = jnp.minimum(courant, 0.0)
    size = jnp.abs(courant)
    slope = 0.5 * size * (1.0 - size)
    return c_minus, c_minus + slope, slope


def window(width, groups, own, edges, outs, scratch):
    ck, cl, ct, mx, fl, obs, mw, cw = own
    final, grad, grad_left, grad_right = outs
    (
        q, temp, lon_code, lat_code, cx, cx_minus, cx_both, cx_slope, cy, cy_minus, cy_both, cy_slope,
        inv, elim, ratio, obs_w, mw_w, force,
    ) = scratch
    lane, col_w = (lane_ids(), col_ids(width))
    count_w = width // LANES
    tracers = PAIR * len(groups)
    offset = groups[0][0]
    static_left, static_right = groups[0][3:5]

    def spread(value, which, place, k):
        if edges is None:
            return value
        north, south = edges[which]
        n_part = pltpu.roll(north[place], (32 + LANES - EDGE * k) % LANES, 1)
        s_part = pltpu.roll(south(place), (64 + LANES - EDGE * k) % LANES, 1)
        top = pltpu.roll(value[:, LANES:], 32, 1)
        low = pltpu.roll(value[:, :LANES], 80, 1)
        outer = jnp.where(lane < 48, n_part, jnp.where(lane < 64, 0.0, s_part))
        inner = jnp.where((lane >= 80) & (lane < 112), low, jnp.where(lane < 112, outer, 0.0))
        return jnp.where(lane < 32, top, inner)

    def squeeze(right, left):
        return jnp.where(col_w < 4, right, left)

    lane_w = lax.broadcasted_iota(jnp.int32, (COLS, width), 1)
    last = lax.axis_index("lat") == lax.axis_size("lat") - 1
    pole = (lane_w == (ROWS - 1 if edges is None else 31)) & last
    carry = [None] * 4
    for level in range(LEVELS):
        def blocks(field, k):
            own_block = spread(field[level], 0, 4 + k, level)
            right = spread(static_right[40 + 8 * k + level], 2, 4 + k, level)
            left = spread(static_left[48 + 8 * k + level], 1, 4 + k, level)
            return [own_block, right, left, squeeze(right, left)]

        for k, value in enumerate(blocks(cl, 0)):
            cx[level, k] = value
            cx_minus[level, k], cx_both[level, k], cx_slope[level, k] = slopes(value)
        for k, value in enumerate(blocks(ct, 1)):
            value = jnp.where(pole, 0.0, value)
            cy[level, k] = value
            cy_minus[level, k], cy_both[level, k], cy_slope[level, k] = slopes(value)
        for k, value in enumerate(blocks(mx, 2)):
            coupling = value if level < LEVELS - 1 else jnp.zeros_like(value)
            pivot = 1.0 + coupling
            if level > 0:
                above, above_ratio = carry[k]
                pivot = pivot + above - above * above_ratio
            inverse = 1.0 / pivot
            inv[level, k] = inverse
            ratio[level, k] = coupling * inverse
            elim[level, k] = above * inverse if level > 0 else jnp.zeros_like(value)
            carry[k] = (coupling, coupling * inverse)

    for substep in range(SUBSTEPS):
        for tracer in range(tracers):
            k = substep * TRACERS + offset + tracer
            obs_w[substep * tracers + tracer] = spread(obs[k], 0, 23 + k // 8, k % 8)
    for tracer in range(tracers):
        mw_w[tracer] = spread(mw[offset + tracer], 0, 25, offset + tracer)

    def put_codes(substep, row, blocks, lat_blocks):
        for k, value in enumerate(blocks):
            lon_code[substep, row, k] = value - jnp.where(value >= 6.0, 6.0, jnp.where(value >= 3.0, 3.0, 0.0))
        for k, value in enumerate(lat_blocks):
            lat_code[substep, row, k] = value

    for first, from_left, from_right, _, _ in groups:
        @pl.loop(0, PAIR)
        def _(within):
            for level in range(LEVELS):
                part = within * LEVELS + level
                row = (first - offset) * LEVELS + part
                whole = first * LEVELS + part
                place = first + within
                q[row, 0] = spread(ck[whole], 0, place, level)
                q[row, 1] = spread(from_right[part], 2, place, level)
                q[row, 2] = spread(from_left[part], 1, place, level)

                def tail(value, which, s):
                    return spread(value, which, 7 + s * TRACERS + place, level)

                mine = [tail(fl[s * STATE + whole].astype(jnp.float32), 0, s) for s in range(SUBSTEPS)]
                l_a, l_b = (from_left[HALF + part], from_left[2 * HALF + part])
                r_a = from_right[HALF + part]
                r_b = from_right[2 * HALF + within * 4 + level % 4]
                if level >= 4:
                    r_b = pltpu.roll(r_b, 4, 0)
                one = [mine[0], tail(r_a, 2, 0), tail(l_a, 1, 0)]
                put_codes(0, row, one, one)
                two = [mine[1], tail(r_b, 2, 1), tail(l_b, 1, 1)]
                put_codes(1, row, two, [mine[1], squeeze(two[1], two[2])])
                three = [
                    mine[2], squeeze(tail(pltpu.roll(r_a, 2, 0), 2, 2), tail(pltpu.roll(l_b, 5, 0), 1, 2))
                ]
                put_codes(2, row, three, three)
                four = [mine[3], tail(pltpu.roll(l_a, 7, 0), 1, 3)]
                put_codes(3, row, four, [mine[3]])

    def ring(slots, read):
        return jnp.concatenate([read(k) for k in slots], axis=0)

    def lon_sweep(substep, row, level, slots, pieces, back):
        code_slots = slots if len(slots) == 3 else (0, 1)
        out = []
        for chunk in range(len(pieces)):
            at = slice(chunk * LANES, (chunk + 1) * LANES)
            value = jnp.concatenate(pieces[chunk], axis=0)
            code = ring(code_slots, lambda k: lon_code[substep, row, k, :, at])
            c, c_minus, c_both, slope = [ring(slots, lambda k: f[level, k, :, at]) for f in (cx, cx_minus, cx_both, cx_slope)]
            first, second = weights(code, 1.0, 2.0, c_minus, c_both, slope)
            value = (sweep_back if back else sweep)(value, c, first, second, 0)
            out.append([value[n * COLS : (n + 1) * COLS] for n in range(len(slots))])
        return out

    def lat_weights(substep, row, level, code_slot, slot):
        return weights(
            lat_code[substep, row, code_slot], 3.0, 6.0, cy_minus[level, slot], cy_both[level, slot], cy_slope[level, slot]
        )

    def forward(substep, slots, out_slots):
        @pl.loop(0, tracers)
        def _(tracer):
            above = {}
            for level in range(LEVELS):
                row = tracer * LEVELS + level
                pieces = [
                    [q[row, k, :, chunk * LANES : (chunk + 1) * LANES] for k in slots] for chunk in range(count_w)
                ]
                pieces = lon_sweep(substep, row, level, slots, pieces, False)
                blocks = {k: jnp.concatenate([piece[n] for piece in pieces], axis=1) for n, k in enumerate(slots)}
                if substep == 1:
                    blocks[3] = squeeze(blocks[1], blocks[2])
                for slot in out_slots:
                    code_slot = 1 if slot == 3 else slot
                    first, second = lat_weights(substep, row, level, code_slot, slot)
                    value = sweep(blocks[slot], cy[level, slot], first, second, 1)
                    value = value * inv[level, slot]
                    if level > 0:
                        value = value + elim[level, slot] * above[slot]
                    above[slot] = value
                    temp[row, slot] = value
            for slot in out_slots:
                value = above[slot]
                column = cw[LEVELS - 1] * value
                for level in range(LEVELS - 1, -1, -1):
                    row = tracer * LEVELS + level
                    if level < LEVELS - 1:
                        value = temp[row, slot] + ratio[level, slot] * value
                        column = column + cw[level] * value
                    if substep == SUBSTEPS - 1:
                        final[row] = value
                    else:
                        q[row, slot] = value
                if slot == 0:
                    at = substep * tracers + tracer
                    force[at] = mw_w[tracer] * (column - obs_w[at])

    def backward(substep, slots, out_slots):
        @pl.loop(0, tracers)
        def _(tracer):
            for slot in slots:
                for level in range(LEVELS):
                    row = tracer * LEVELS + level
                    if slot == 0:
                        value = cw[level] * force[substep * tracers + tracer]
                        if substep < SUBSTEPS - 1:
                            value = value + q[row, slot]
                    else:
                        value = q[row, slot]
                    value = value * inv[level, slot]
                    if level > 0:
                        value = value + elim[level, slot] * above
                    above = value
                    temp[row, slot] = value
            below = {}
            for level in range(LEVELS - 1, -1, -1):
                row = tracer * LEVELS + level
                blocks = {}
                for slot in slots:
                    code_slot = 1 if slot == 3 else slot
                    value = temp[row, slot]
                    if level < LEVELS - 1:
                        value = value + ratio[level, slot] * below[slot]
                    below[slot] = value
                    first, second = lat_weights(substep, row, level, code_slot, slot)
                    blocks[slot] = sweep_back(value, cy[level, slot], first, second, 1)
                if substep == SUBSTEPS - 1:
                    blocks[3] = jnp.zeros_like(blocks[0])
                if substep == 1:
                    blocks[1] = jnp.where(col_w < 4, blocks[3], 0.0)
                    blocks[2] = jnp.where(col_w < 4, 0.0, blocks[3])
                pieces = [
                    [blocks[k][:, chunk * LANES : (chunk + 1) * LANES] for k in out_slots] for chunk in range(count_w)
                ]
                pieces = lon_sweep(substep, row, level, out_slots, pieces, True)
                for chunk in range(count_w):
                    at = slice(chunk * LANES, (chunk + 1) * LANES)
                    for n, k in enumerate(out_slots):
                        if substep == 0:
                            (grad, grad_right, grad_left)[k][row, :, at] = pieces[chunk][n]
                        else:
                            q[row, k, :, at] = pieces[chunk][n]

    three, two = ((0, 1, 2), (0, 3))
    forward(0, three, three)
    forward(1, three, two)
    forward(2, two, two)
    forward(3, two, (0,))
    backward(3, (0,), two)
    backward(2, two, two)
    backward(1, two, three)
    backward(0, three, three)


def keep_inner(value):
    lane = lax.broadcasted_iota(jnp.int32, (COLS, ROWS), 1)
    return jnp.where((lane >= EDGE) & (lane < ROWS - EDGE), value, 0.0)


def main_first(*refs):
    own, (left_a, right_a), outs, scratch = (refs[:8], refs[8:10], refs[10:14], refs[14:])
    window(ROWS, [(0, left_a, right_a, left_a, right_a)], own, None, outs, scratch)
    for ref in outs[2:]:
        @pl.loop(0, HALF)
        def _(row):
            ref[row] = keep_inner(ref[row])


def main_second(*refs):
    own, (left_a, right_a, left_b, right_b), before, outs, scratch = (
        refs[:8], refs[8:12], refs[12:16], refs[16:20], refs[20:]
    )
    parts = [ref.at[HALF:STATE] for ref in outs]
    for ref, old in zip(outs, before):
        ref[0:HALF] = old[...]
    window(ROWS, [(PAIR, left_b, right_b, left_a, right_a)], own, None, parts, scratch)
    for ref in outs[2:]:
        @pl.loop(HALF, STATE)
        def _(row):
            ref[row] = keep_inner(ref[row])


def strip(*refs):
    own, (left_a, right_a, left_b, right_b, north, south, corner_l, corner_r), (main_final, main_grad) = (
        refs[:8], refs[8:16], refs[16:18]
    )
    final, grad, pack_left, pack_right = refs[18:22]
    outs, scratch = (refs[22:26], refs[26:])
    edges = (
        (north, lambda k: south[k]),
        (corner_l, lambda k: corner_l[CORNER + k]),
        (corner_r, lambda k: corner_r[CORNER + k]),
    )
    groups = [(0, left_a, right_a, left_a, right_a), (PAIR, left_b, right_b, left_a, right_a)]
    window(LANES, groups, own, edges, outs, scratch)
    lane = lane_ids()

    @pl.loop(0, STATE)
    def _(row):
        for target, source, value in ((final, main_final, outs[0][row]), (grad, main_grad, outs[1][row])):
            low = pltpu.roll(value, 48, 1)
            top = pltpu.roll(value, 96, 1)
            target[row, :, :LANES] = jnp.where(lane < EDGE, low, source[row, :, :LANES])
            target[row, :, LANES:] = jnp.where(lane >= LANES - EDGE, top, source[row, :, LANES:])

    for level in range(LEVELS):
        for target, source in ((pack_left, outs[2]), (pack_right, outs[3])):
            packed = jnp.zeros((COLS, LANES), jnp.float32)
            for tracer in range(TRACERS):
                value = source[tracer * LEVELS + level]
                start = 32 * tracer
                top = pltpu.roll(value, (start + LANES - 16) % LANES, 1)
                low = pltpu.roll(value, (start + 16 + LANES - 80) % LANES, 1)
                packed = jnp.where(lane >= start, jnp.where(lane < start + 16, top, low), packed)
            target[level] = packed


def finish(grad, from_right, from_left, edge_right, edge_left, out):
    lane = lane_ids()
    for level in range(LEVELS):
        packed = edge_right[level] + edge_left[level]
        for tracer in range(TRACERS):
            row = tracer * LEVELS + level
            start = 32 * tracer
            top = pltpu.roll(packed, (2 * LANES - 16 - start) % LANES, 1)
            low = pltpu.roll(packed, (2 * LANES - 16 - start) % LANES, 1)
            total = grad[row] + from_right[row] + from_left[row]
            out[row, :, :LANES] = total[:, :LANES] + jnp.where(lane < EDGE, low, 0.0)
            out[row, :, LANES:] = total[:, LANES:] + jnp.where(lane >= LANES - EDGE, top, 0.0)


def spec(count, space=pltpu.VMEM):
    return [pl.BlockSpec(memory_space=space)] * count


def scratch_for(width, tracers):
    rows = tracers * LEVELS
    sizes = [(rows, 4)] * 2 + [(SUBSTEPS, rows, 3)] * 2 + [(LEVELS, 4)] * 11 + [(SUBSTEPS * tracers,), (tracers,), (SUBSTEPS * tracers,)]
    return [pltpu.VMEM(size + (COLS, width), jnp.float32) for size in sizes]


def shards(
    checkpoint, courant_lon, courant_lat, mixing, limiter_flags, column_weights, observations, misfit_weight
):
    def block(rows, lanes=ROWS):
        return jax.ShapeDtypeStruct((rows, COLS, lanes), jnp.float32)

    def call(kernel, name, outs, in_specs, operands, scratch=(), cost=0):
        return pl.pallas_call(
            kernel,
            out_shape=tuple(outs),
            in_specs=in_specs,
            out_specs=tuple(spec(len(outs))),
            scratch_shapes=list(scratch),
            compiler_params=pltpu.CompilerParams(vmem_limit_bytes=LIMIT),
            name=name,
        )(*operands)

    lat, lon = (lax.axis_size("lat"), lax.axis_size("lon"))
    east = [(i, (i + 1) % lon) for i in range(lon)]
    west = [(j, i) for i, j in east]
    up = [(i, i + 1) for i in range(lat - 1)]
    down = [(j, i) for i, j in up]
    own = (
        checkpoint.reshape((STATE, COLS, ROWS)),
        courant_lon,
        courant_lat,
        mixing,
        limiter_flags.reshape((SUBSTEPS * STATE, COLS, ROWS)),
        observations.reshape((SUBSTEPS * TRACERS, COLS, ROWS)),
        misfit_weight,
    )
    copies = [pltpu.VMEM(value.shape, value.dtype) for value in own]
    right_a, right_b, left_a, left_b, to_north, to_south = call(
        pack,
        "pack",
        (block(72), block(48), block(64), block(40), block(26, LANES), block(26, LANES)),
        spec(7, pltpu.HBM),
        own,
        copies + [pltpu.SemaphoreType.DMA((7,))],
    )
    from_left_a = lax.ppermute(right_a, "lon", east)
    from_right_a = lax.ppermute(left_a, "lon", west)
    south = lax.ppermute(to_north, "lat", up)
    north = lax.ppermute(to_south, "lat", down)
    from_left_b = lax.ppermute(right_b, "lon", east)
    from_right_b = lax.ppermute(left_b, "lon", west)
    corner = jnp.concatenate([north[:CORNER], south[:CORNER]], axis=0)
    corner_l = lax.ppermute(corner, "lon", east)
    corner_r = lax.ppermute(corner, "lon", west)
    smem = spec(1, pltpu.SMEM)
    owned = own + (column_weights,)
    first = call(
        main_first, "main_first", [block(HALF)] * 4, spec(7) + smem + spec(2),
        owned + (from_left_a, from_right_a), scratch_for(ROWS, PAIR),
    )
    main_final, main_grad, grad_left, grad_right = call(
        main_second, "main_second", [block(STATE)] * 4, spec(7) + smem + spec(8),
        owned + (from_left_a, from_right_a, from_left_b, from_right_b) + tuple(first), scratch_for(ROWS, PAIR),
    )
    from_right = lax.ppermute(grad_left, "lon", west)
    from_left = lax.ppermute(grad_right, "lon", east)
    narrow = [pltpu.VMEM((STATE, COLS, LANES), jnp.float32)] * 4
    final, grad, pack_left, pack_right = call(
        strip, "strip", [block(STATE)] * 2 + [block(LEVELS, LANES)] * 2, spec(7) + smem + spec(10),
        owned + (from_left_a, from_right_a, from_left_b, from_right_b, north, south, corner_l, corner_r, main_final, main_grad),
        narrow + scratch_for(LANES, TRACERS),
    )
    edge_right = lax.ppermute(pack_left, "lon", west)
    edge_left = lax.ppermute(pack_right, "lon", east)
    (grad,) = call(finish, "finish", [block(STATE)], spec(5), (grad, from_right, from_left, edge_right, edge_left))
    return (final.reshape(checkpoint.shape), grad.reshape(checkpoint.shape))


def solution(mesh):
    return jax.shard_map(
        shards,
        mesh=mesh,
        in_specs=(
            P(None, None, "lon", "lat"),
            P(None, "lon", "lat"),
            P(None, "lon", "lat"),
            P(None, "lon", "lat"),
            P(None, None, None, "lon", "lat"),
            P(),
            P(None, None, "lon", "lat"),
            P(None, "lon", "lat"),
        ),
        out_specs=(P(None, None, "lon", "lat"), P(None, None, "lon", "lat")),
        check_vma=False,
    )
```

```python
import jax
import jax.numpy as jnp
from jax import lax
from jax.experimental import pallas as pl
from jax.experimental.pallas import tpu as pltpu
from jax.sharding import PartitionSpec as P

TRACERS, LEVELS, SUBSTEPS = 4, 8, 4
PAIR = 2
TOGETHER = {1: 2, 2: 1}
COLS, ROWS, EDGE, LANES = 8, 256, 16, 128
STATE = TRACERS * LEVELS
HALF = PAIR * LEVELS
LIMIT = 24 * 1024 * 1024
CORNER = 23


def lane_ids():
    return lax.broadcasted_iota(jnp.int32, (COLS, LANES), 1)


def col_ids(lanes=LANES):
    return lax.broadcasted_iota(jnp.int32, (COLS, lanes), 0)


def pack(*refs):
    hbm, own, (right_a, right_b, left_a, left_b, to_north, to_south), sems = (refs[:7], refs[7:14], refs[14:20], refs[20])
    copies = [pltpu.make_async_copy(hbm[k], own[k], sems.at[k]) for k in range(7)]
    for copy in copies:
        copy.start()
    for copy in copies:
        copy.wait()
    ck, cl, ct, mx, fl, obs, mw = own
    lane, col = (lane_ids(), col_ids(ROWS))
    for half, (to_right, to_left) in enumerate(((right_a, left_a), (right_b, left_b))):
        to_right[0:HALF] = ck[half * HALF : (half + 1) * HALF]
        to_left[0:HALF] = ck[half * HALF : (half + 1) * HALF]

        @pl.loop(0, PAIR)
        def _(tracer):
            for level in range(LEVELS):
                row = tracer * LEVELS + level
                one, two, three, four = [
                    fl[s * STATE + half * HALF + row].astype(jnp.float32) for s in range(SUBSTEPS)
                ]
                to_right[HALF + row] = jnp.where(col >= 1, one, pltpu.roll(four, 1, 0))
                to_right[2 * HALF + row] = jnp.where(col >= 3, two, pltpu.roll(three, 3, 0))
                to_left[HALF + row] = jnp.where(col < 6, one, pltpu.roll(three, 6, 0))
                if level < 4:
                    other = fl[STATE + half * HALF + row + 4].astype(jnp.float32)
                    to_left[2 * HALF + tracer * 4 + level] = jnp.where(col < 4, two, pltpu.roll(other, 4, 0))

    for k, field in enumerate((cl, ct, mx)):
        right_a[3 * HALF + 8 * k : 3 * HALF + 8 * k + 8] = field[...]
        left_a[40 + 8 * k : 48 + 8 * k] = field[...]

    def strips(place, read, count):
        north = jnp.zeros((COLS, LANES), jnp.float32)
        south = north
        for k in range(count):
            whole = read(k)
            here = lane // EDGE
            north = jnp.where(here == (k + 1) % 8, pltpu.roll(whole[:, LANES:], (EDGE * (k + 2)) % LANES, 1), north)
            south = jnp.where(here == k, pltpu.roll(whole[:, :LANES], EDGE * k, 1), south)
        to_north[place] = north
        to_south[place] = south

    @pl.loop(0, TRACERS)
    def _(tracer):
        strips(tracer, lambda k: ck[tracer * LEVELS + k], LEVELS)

    for place, field in ((4, cl), (5, ct), (6, mx)):
        strips(place, lambda k, field=field: field[k], LEVELS)

    @pl.loop(0, SUBSTEPS * TRACERS)
    def _(block):
        strips(7 + block, lambda k: fl[block * LEVELS + k].astype(jnp.float32), LEVELS)

    for half in range(2):
        strips(23 + half, lambda k, half=half: obs[half * 8 + k], 8)
    strips(25, lambda k: mw[k], TRACERS)


def behind(value, axis):
    return pltpu.roll(value, 1, axis)


def ahead(value, axis):
    return pltpu.roll(value, value.shape[axis] - 1, axis)


def weights(branch, low, high, c_minus, c_both, slope):
    first = jnp.where(branch >= high, c_minus, jnp.where(branch >= low, c_both, c_minus))
    return first, jnp.where(branch >= high, slope, 0.0)


def sweep(value, courant, first, second, axis):
    step = ahead(value, axis) - value
    farther = jnp.where(courant >= 0.0, behind(step, axis), ahead(step, axis))
    flux = courant * value + first * step + second * farther
    return value - flux + behind(flux, axis)


def sweep_back(value, courant, first, second, axis):
    step = ahead(value, axis) - value
    reach = second * step
    forward = jnp.where(courant >= 0.0, reach, 0.0)
    total = first * step + ahead(forward, axis) + behind(reach - forward, axis)
    return value + courant * step + behind(total, axis) - total


def slopes(courant):
    c_minus = jnp.minimum(courant, 0.0)
    size = jnp.abs(courant)
    slope = 0.5 * size * (1.0 - size)
    return c_minus, c_minus + slope, slope


def window(width, groups, own, edges, outs, scratch):
    ck, cl, ct, mx, fl, obs, mw, cw = own
    final, grad, grad_left, grad_right = outs
    (
        q, temp, lon_code, lat_code, cx, cx_minus, cx_both, cx_slope, cy, cy_minus, cy_both, cy_slope,
        inv, elim, ratio, obs_w, mw_w, force,
    ) = scratch
    lane, col_w = (lane_ids(), col_ids(width))
    strip_of = lane // EDGE
    count_w = width // LANES
    together = TOGETHER[count_w]
    tracers = PAIR * len(groups)
    offset = groups[0][0]
    static_left, static_right = groups[0][3:5]

    def spread(value, which, place, k):
        if edges is None:
            return value
        north, south = edges[which]
        halo = pltpu.roll(jnp.where(strip_of == k, north[place], south(place)), (96 + LANES - EDGE * k) % LANES, 1)
        top = pltpu.roll(value[:, LANES:], 96, 1)
        inner = jnp.where(lane < 32, value[:, :LANES], jnp.where(lane < 64, 0.0, top))
        return jnp.where(lane < 96, inner, halo)

    def squeeze(right, left):
        return jnp.where(col_w < 4, right, left)

    lane_w = lax.broadcasted_iota(jnp.int32, (COLS, width), 1)
    last = lax.axis_index("lat") == lax.axis_size("lat") - 1
    pole = (lane_w == (ROWS - 1 if edges is None else 95)) & last
    carry = [None] * 4
    for level in range(LEVELS):
        def blocks(field, k):
            own_block = spread(field[level], 0, 4 + k, level)
            right = spread(static_right[40 + 8 * k + level], 2, 4 + k, level)
            left = spread(static_left[48 + 8 * k + level], 1, 4 + k, level)
            return [own_block, right, left, squeeze(right, left)]

        for k, value in enumerate(blocks(cl, 0)):
            cx[level, k] = value
            cx_minus[level, k], cx_both[level, k], cx_slope[level, k] = slopes(value)
        for k, value in enumerate(blocks(ct, 1)):
            value = jnp.where(pole, 0.0, value)
            cy[level, k] = value
            cy_minus[level, k], cy_both[level, k], cy_slope[level, k] = slopes(value)
        for k, value in enumerate(blocks(mx, 2)):
            coupling = value if level < LEVELS - 1 else jnp.zeros_like(value)
            pivot = 1.0 + coupling
            if level > 0:
                above, above_ratio = carry[k]
                pivot = pivot + above - above * above_ratio
            inverse = 1.0 / pivot
            inv[level, k] = inverse
            ratio[level, k] = coupling * inverse
            elim[level, k] = above * inverse if level > 0 else jnp.zeros_like(value)
            carry[k] = (coupling, coupling * inverse)

    for substep in range(SUBSTEPS):
        for tracer in range(tracers):
            k = substep * TRACERS + offset + tracer
            obs_w[substep * tracers + tracer] = spread(obs[k], 0, 23 + k // 8, k % 8)
    for tracer in range(tracers):
        mw_w[tracer] = spread(mw[offset + tracer], 0, 25, offset + tracer)

    def put_codes(substep, row, blocks, lat_blocks):
        for k, value in enumerate(blocks):
            lon_code[substep, row, k] = value - jnp.where(value >= 6.0, 6.0, jnp.where(value >= 3.0, 3.0, 0.0))
        for k, value in enumerate(lat_blocks):
            lat_code[substep, row, k] = value

    for first, from_left, from_right, _, _ in groups:
        @pl.loop(0, PAIR)
        def _(within):
            for level in range(LEVELS):
                part = within * LEVELS + level
                row = (first - offset) * LEVELS + part
                whole = first * LEVELS + part
                place = first + within
                q[row, 0] = spread(ck[whole], 0, place, level)
                q[row, 1] = spread(from_right[part], 2, place, level)
                q[row, 2] = spread(from_left[part], 1, place, level)

                def tail(value, which, s):
                    return spread(value, which, 7 + s * TRACERS + place, level)

                mine = [tail(fl[s * STATE + whole].astype(jnp.float32), 0, s) for s in range(SUBSTEPS)]
                l_a, l_b = (from_left[HALF + part], from_left[2 * HALF + part])
                r_a = from_right[HALF + part]
                r_b = from_right[2 * HALF + within * 4 + level % 4]
                if level >= 4:
                    r_b = pltpu.roll(r_b, 4, 0)
                one = [mine[0], tail(r_a, 2, 0), tail(l_a, 1, 0)]
                put_codes(0, row, one, one)
                two = [mine[1], tail(r_b, 2, 1), tail(l_b, 1, 1)]
                put_codes(1, row, two, [mine[1], squeeze(two[1], two[2])])
                three = [
                    mine[2], squeeze(tail(pltpu.roll(r_a, 2, 0), 2, 2), tail(pltpu.roll(l_b, 5, 0), 1, 2))
                ]
                put_codes(2, row, three, three)
                four = [mine[3], tail(pltpu.roll(l_a, 7, 0), 1, 3)]
                put_codes(3, row, four, [mine[3]])

    def ring(slots, read):
        return jnp.concatenate([read(k) for k in slots], axis=0)

    def lon_sweep(substep, row, level, slots, pieces, back):
        code_slots = slots if len(slots) == 3 else (0, 1)
        out = []
        for chunk in range(len(pieces)):
            at = slice(chunk * LANES, (chunk + 1) * LANES)
            value = jnp.concatenate(pieces[chunk], axis=0)
            code = ring(code_slots, lambda k: lon_code[substep, row, k, :, at])
            c, c_minus, c_both, slope = [ring(slots, lambda k: f[level, k, :, at]) for f in (cx, cx_minus, cx_both, cx_slope)]
            first, second = weights(code, 1.0, 2.0, c_minus, c_both, slope)
            value = (sweep_back if back else sweep)(value, c, first, second, 0)
            out.append([value[n * COLS : (n + 1) * COLS] for n in range(len(slots))])
        return out

    def lat_weights(substep, row, level, code_slot, slot):
        return weights(
            lat_code[substep, row, code_slot], 3.0, 6.0, cy_minus[level, slot], cy_both[level, slot], cy_slope[level, slot]
        )

    def forward(substep, slots, out_slots):
        @pl.loop(0, tracers // together)
        def _(batch):
            members = [batch * together + n for n in range(together)]
            above = {}
            for level in range(LEVELS):
                for n, tracer in enumerate(members):
                    row = tracer * LEVELS + level
                    pieces = [
                        [q[row, k, :, chunk * LANES : (chunk + 1) * LANES] for k in slots] for chunk in range(count_w)
                    ]
                    pieces = lon_sweep(substep, row, level, slots, pieces, False)
                    blocks = {k: jnp.concatenate([piece[m] for piece in pieces], axis=1) for m, k in enumerate(slots)}
                    if substep == 1:
                        blocks[3] = squeeze(blocks[1], blocks[2])
                    for slot in out_slots:
                        code_slot = 1 if slot == 3 else slot
                        first, second = lat_weights(substep, row, level, code_slot, slot)
                        value = sweep(blocks[slot], cy[level, slot], first, second, 1)
                        value = value * inv[level, slot]
                        if level > 0:
                            value = value + elim[level, slot] * above[n, slot]
                        above[n, slot] = value
                        temp[row, slot] = value
            column = {}
            for level in range(LEVELS - 1, -1, -1):
                for n, tracer in enumerate(members):
                    row = tracer * LEVELS + level
                    for slot in out_slots:
                        value = above[n, slot]
                        if level < LEVELS - 1:
                            value = temp[row, slot] + ratio[level, slot] * value
                            above[n, slot] = value
                        if slot == 0:
                            part = cw[level] * value
                            column[n] = part if level == LEVELS - 1 else column[n] + part
                        if substep == SUBSTEPS - 1:
                            final[row] = value
                        else:
                            q[row, slot] = value
            for n, tracer in enumerate(members):
                at = substep * tracers + tracer
                force[at] = mw_w[tracer] * (column[n] - obs_w[at])

    def backward(substep, slots, out_slots):
        @pl.loop(0, tracers // together)
        def _(batch):
            members = [batch * together + n for n in range(together)]
            above = {}
            for level in range(LEVELS):
                for n, tracer in enumerate(members):
                    row = tracer * LEVELS + level
                    for slot in slots:
                        if slot == 0:
                            value = cw[level] * force[substep * tracers + tracer]
                            if substep < SUBSTEPS - 1:
                                value = value + q[row, slot]
                        else:
                            value = q[row, slot]
                        value = value * inv[level, slot]
                        if level > 0:
                            value = value + elim[level, slot] * above[n, slot]
                        above[n, slot] = value
                        temp[row, slot] = value
            below = {}
            for level in range(LEVELS - 1, -1, -1):
                for n, tracer in enumerate(members):
                    row = tracer * LEVELS + level
                    blocks = {}
                    for slot in slots:
                        code_slot = 1 if slot == 3 else slot
                        value = temp[row, slot]
                        if level < LEVELS - 1:
                            value = value + ratio[level, slot] * below[n, slot]
                        below[n, slot] = value
                        first, second = lat_weights(substep, row, level, code_slot, slot)
                        blocks[slot] = sweep_back(value, cy[level, slot], first, second, 1)
                    if substep == SUBSTEPS - 1:
                        blocks[3] = jnp.zeros_like(blocks[0])
                    if substep == 1:
                        blocks[1] = jnp.where(col_w < 4, blocks[3], 0.0)
                        blocks[2] = jnp.where(col_w < 4, 0.0, blocks[3])
                    pieces = [
                        [blocks[k][:, chunk * LANES : (chunk + 1) * LANES] for k in out_slots] for chunk in range(count_w)
                    ]
                    pieces = lon_sweep(substep, row, level, out_slots, pieces, True)
                    for chunk in range(count_w):
                        at = slice(chunk * LANES, (chunk + 1) * LANES)
                        for m, k in enumerate(out_slots):
                            if substep == 0:
                                (grad, grad_right, grad_left)[k][row, :, at] = pieces[chunk][m]
                            else:
                                q[row, k, :, at] = pieces[chunk][m]

    three, two = ((0, 1, 2), (0, 3))
    forward(0, three, three)
    forward(1, three, two)
    forward(2, two, two)
    forward(3, two, (0,))
    backward(3, (0,), two)
    backward(2, two, two)
    backward(1, two, three)
    backward(0, three, three)


def keep_inner(value):
    lane = lax.broadcasted_iota(jnp.int32, (COLS, ROWS), 1)
    return jnp.where((lane >= EDGE) & (lane < ROWS - EDGE), value, 0.0)


def main_first(*refs):
    own, (left_a, right_a), outs, scratch = (refs[:8], refs[8:10], refs[10:14], refs[14:])
    window(ROWS, [(0, left_a, right_a, left_a, right_a)], own, None, outs, scratch)
    for ref in outs[2:]:
        @pl.loop(0, HALF)
        def _(row):
            ref[row] = keep_inner(ref[row])


def main_second(*refs):
    own, (left_a, right_a, left_b, right_b), before, outs, scratch = (
        refs[:8], refs[8:12], refs[12:16], refs[16:20], refs[20:]
    )
    parts = [ref.at[HALF:STATE] for ref in outs]
    for ref, old in zip(outs, before):
        ref[0:HALF] = old[...]
    window(ROWS, [(PAIR, left_b, right_b, left_a, right_a)], own, None, parts, scratch)
    for ref in outs[2:]:
        @pl.loop(HALF, STATE)
        def _(row):
            ref[row] = keep_inner(ref[row])


def strip(*refs):
    own, (left_a, right_a, left_b, right_b, north, south, corner_l, corner_r), (main_final, main_grad) = (
        refs[:8], refs[8:16], refs[16:18]
    )
    final, grad, pack_left, pack_right = refs[18:22]
    outs, scratch = (refs[22:26], refs[26:])
    edges = (
        (north, lambda k: south[k]),
        (corner_l, lambda k: corner_l[CORNER + k]),
        (corner_r, lambda k: corner_r[CORNER + k]),
    )
    groups = [(0, left_a, right_a, left_a, right_a), (PAIR, left_b, right_b, left_a, right_a)]
    window(LANES, groups, own, edges, outs, scratch)
    lane = lane_ids()

    @pl.loop(0, STATE)
    def _(row):
        for target, source, value in ((final, main_final, outs[0][row]), (grad, main_grad, outs[1][row])):
            top = pltpu.roll(value, 32, 1)
            target[row, :, :LANES] = jnp.where(lane < EDGE, value, source[row, :, :LANES])
            target[row, :, LANES:] = jnp.where(lane >= LANES - EDGE, top, source[row, :, LANES:])

    for level in range(LEVELS):
        for target, source in ((pack_left, outs[2]), (pack_right, outs[3])):
            packed = jnp.zeros((COLS, LANES), jnp.float32)
            for tracer in range(TRACERS):
                value = source[tracer * LEVELS + level]
                start = 32 * tracer
                top = pltpu.roll(value, (start + LANES - 80) % LANES, 1)
                low = pltpu.roll(value, (start + 16) % LANES, 1)
                packed = jnp.where(lane >= start, jnp.where(lane < start + 16, top, low), packed)
            target[level] = packed


def finish(grad, from_right, from_left, edge_right, edge_left, out):
    lane = lane_ids()
    for level in range(LEVELS):
        packed = edge_right[level] + edge_left[level]
        for tracer in range(TRACERS):
            row = tracer * LEVELS + level
            start = 32 * tracer
            edge = pltpu.roll(packed, (2 * LANES - 16 - start) % LANES, 1)
            total = grad[row] + from_right[row] + from_left[row]
            out[row, :, :LANES] = total[:, :LANES] + jnp.where(lane < EDGE, edge, 0.0)
            out[row, :, LANES:] = total[:, LANES:] + jnp.where(lane >= LANES - EDGE, edge, 0.0)


def spec(count, space=pltpu.VMEM):
    return [pl.BlockSpec(memory_space=space)] * count


def scratch_for(width, tracers):
    rows = tracers * LEVELS
    sizes = [(rows, 4)] * 2 + [(SUBSTEPS, rows, 3)] * 2 + [(LEVELS, 4)] * 11 + [(SUBSTEPS * tracers,), (tracers,), (SUBSTEPS * tracers,)]
    return [pltpu.VMEM(size + (COLS, width), jnp.float32) for size in sizes]


def shards(
    checkpoint, courant_lon, courant_lat, mixing, limiter_flags, column_weights, observations, misfit_weight
):
    def block(rows, lanes=ROWS):
        return jax.ShapeDtypeStruct((rows, COLS, lanes), jnp.float32)

    def call(kernel, name, outs, in_specs, operands, scratch=(), cost=0):
        return pl.pallas_call(
            kernel,
            out_shape=tuple(outs),
            in_specs=in_specs,
            out_specs=tuple(spec(len(outs))),
            scratch_shapes=list(scratch),
            compiler_params=pltpu.CompilerParams(vmem_limit_bytes=LIMIT),
            name=name,
        )(*operands)

    lat, lon = (lax.axis_size("lat"), lax.axis_size("lon"))
    east = [(i, (i + 1) % lon) for i in range(lon)]
    west = [(j, i) for i, j in east]
    up = [(i, i + 1) for i in range(lat - 1)]
    down = [(j, i) for i, j in up]
    own = (
        checkpoint.reshape((STATE, COLS, ROWS)),
        courant_lon,
        courant_lat,
        mixing,
        limiter_flags.reshape((SUBSTEPS * STATE, COLS, ROWS)),
        observations.reshape((SUBSTEPS * TRACERS, COLS, ROWS)),
        misfit_weight,
    )
    packed = call(
        pack,
        "pack",
        [jax.ShapeDtypeStruct(value.shape, value.dtype) for value in own]
        + [block(72), block(48), block(64), block(40), block(26, LANES), block(26, LANES)],
        spec(7, pltpu.HBM),
        own,
        [pltpu.SemaphoreType.DMA((7,))],
    )
    own, (right_a, right_b, left_a, left_b, to_north, to_south) = (tuple(packed[:7]), packed[7:])
    from_left_a = lax.ppermute(right_a, "lon", east)
    from_right_a = lax.ppermute(left_a, "lon", west)
    south = lax.ppermute(to_north, "lat", up)
    north = lax.ppermute(to_south, "lat", down)
    from_left_b = lax.ppermute(right_b, "lon", east)
    left_b, from_right_a = lax.optimization_barrier((left_b, from_right_a))
    from_right_b = lax.ppermute(left_b, "lon", west)
    smem = spec(1, pltpu.SMEM)
    owned = own + (column_weights,)
    first = call(
        main_first, "main_first", [block(HALF)] * 4, spec(7) + smem + spec(2),
        owned + (from_left_a, from_right_a), scratch_for(ROWS, PAIR),
    )
    first, north, south = lax.optimization_barrier((tuple(first), north, south))
    corner = jnp.concatenate([north[:CORNER], south[:CORNER]], axis=0)
    first, corner = lax.optimization_barrier((first, corner))
    corner_l = lax.ppermute(corner, "lon", east)
    corner_r = lax.ppermute(corner, "lon", west)
    main_final, main_grad, grad_left, grad_right = call(
        main_second, "main_second", [block(STATE)] * 4, spec(7) + smem + spec(8),
        owned + (from_left_a, from_right_a, from_left_b, from_right_b) + tuple(first), scratch_for(ROWS, PAIR),
    )
    from_right = lax.ppermute(grad_left, "lon", west)
    from_left = lax.ppermute(grad_right, "lon", east)
    narrow = [pltpu.VMEM((STATE, COLS, LANES), jnp.float32)] * 4
    final, grad, pack_left, pack_right = call(
        strip, "strip", [block(STATE)] * 2 + [block(LEVELS, LANES)] * 2, spec(7) + smem + spec(10),
        owned + (from_left_a, from_right_a, from_left_b, from_right_b, north, south, corner_l, corner_r, main_final, main_grad),
        narrow + scratch_for(LANES, TRACERS),
    )
    edge_right = lax.ppermute(pack_left, "lon", west)
    edge_left = lax.ppermute(pack_right, "lon", east)
    (grad,) = call(finish, "finish", [block(STATE)], spec(5), (grad, from_right, from_left, edge_right, edge_left))
    return (final.reshape(checkpoint.shape), grad.reshape(checkpoint.shape))


def solution(mesh):
    return jax.shard_map(
        shards,
        mesh=mesh,
        in_specs=(
            P(None, None, "lon", "lat"),
            P(None, "lon", "lat"),
            P(None, "lon", "lat"),
            P(None, "lon", "lat"),
            P(None, None, None, "lon", "lat"),
            P(),
            P(None, None, "lon", "lat"),
            P(None, "lon", "lat"),
        ),
        out_specs=(P(None, None, "lon", "lat"), P(None, None, "lon", "lat")),
        check_vma=False,
    )
```

```python
import functools

import jax
import jax.numpy as jnp
from jax import lax
from jax.experimental import pallas as pl
from jax.experimental.pallas import tpu as pltpu
from jax.sharding import PartitionSpec as P

TRACERS, LEVELS, SUBSTEPS = 4, 8, 4
PAIR = 2
COLS, ROWS, EDGE, LANES = 8, 256, 16, 128
STATE = TRACERS * LEVELS
HALF = PAIR * LEVELS
LIMIT = 24 * 1024 * 1024
PACK_LIMIT = 60 * 1024 * 1024
CORNER = 23


def lane_ids():
    return lax.broadcasted_iota(jnp.int32, (COLS, LANES), 1)


def col_ids(lanes=LANES):
    return lax.broadcasted_iota(jnp.int32, (COLS, lanes), 0)


def fetch(hbm, own, sems):
    copies = [pltpu.make_async_copy(source, target, sems.at[k]) for k, (source, target) in enumerate(zip(hbm, own))]
    for copy in copies:
        copy.start()
    for copy in copies:
        copy.wait()


def pack_lon(*refs):
    hbm, (right_a, right_b, left_a, left_b), own, sems = (refs[:5], refs[6:10], refs[10:15], refs[15])
    fetch(hbm, own, sems)
    ck, cl, ct, mx, fl = own
    col = col_ids(ROWS)
    for half, (to_right, to_left) in enumerate(((right_a, left_a), (right_b, left_b))):
        to_right[0:HALF] = ck[half * HALF : (half + 1) * HALF]
        to_left[0:HALF] = ck[half * HALF : (half + 1) * HALF]

        @pl.loop(0, PAIR)
        def _(tracer):
            for level in range(LEVELS):
                row = tracer * LEVELS + level
                one, two, three, four = [
                    fl[s * STATE + half * HALF + row].astype(jnp.float32) for s in range(SUBSTEPS)
                ]
                to_right[HALF + row] = jnp.where(col >= 1, one, pltpu.roll(four, 1, 0))
                to_right[2 * HALF + row] = jnp.where(col >= 3, two, pltpu.roll(three, 3, 0))
                to_left[HALF + row] = jnp.where(col < 6, one, pltpu.roll(three, 6, 0))
                if level < 4:
                    other = fl[STATE + half * HALF + row + 4].astype(jnp.float32)
                    to_left[2 * HALF + tracer * 4 + level] = jnp.where(col < 4, two, pltpu.roll(other, 4, 0))

    for k, field in enumerate((cl, ct, mx)):
        right_a[3 * HALF + 8 * k : 3 * HALF + 8 * k + 8] = field[...]
        left_a[40 + 8 * k : 48 + 8 * k] = field[...]


def pack_lat(*refs):
    hbm, (to_north, to_south), own, sems = (refs[:7], refs[7:9], refs[9:16], refs[16])
    fetch(hbm, own, sems)
    ck, cl, ct, mx, fl, obs, mw = own
    lane = lane_ids()

    def strips(place, read, count):
        north = jnp.zeros((COLS, LANES), jnp.float32)
        south = north
        for k in range(count):
            whole = read(k)
            here = lane // EDGE
            north = jnp.where(here == (k + 7) % 8, pltpu.roll(whole[:, LANES:], EDGE * k, 1), north)
            south = jnp.where(here == k, pltpu.roll(whole[:, :LANES], EDGE * k, 1), south)
        to_north[place] = north
        to_south[place] = south

    @pl.loop(0, TRACERS)
    def _(tracer):
        strips(tracer, lambda k: ck[tracer * LEVELS + k], LEVELS)

    for place, field in ((4, cl), (5, ct), (6, mx)):
        strips(place, lambda k, field=field: field[k], LEVELS)

    @pl.loop(0, SUBSTEPS * TRACERS)
    def _(block):
        strips(7 + block, lambda k: fl[block * LEVELS + k].astype(jnp.float32), LEVELS)

    for half in range(2):
        strips(23 + half, lambda k, half=half: obs[half * 8 + k], 8)
    strips(25, lambda k: mw[k], TRACERS)


def join(*refs):
    north, south, out = (refs[7], refs[8], refs[9])
    out[0:CORNER] = north[0:CORNER]
    out[CORNER : 2 * CORNER] = south[0:CORNER]


def behind(value, axis):
    return pltpu.roll(value, 1, axis)


def ahead(value, axis):
    return pltpu.roll(value, value.shape[axis] - 1, axis)


def weights(branch, low, high, c_minus, c_both, slope):
    first = jnp.where(branch >= high, c_minus, jnp.where(branch >= low, c_both, c_minus))
    return first, jnp.where(branch >= high, slope, 0.0)


def sweep(value, courant, first, second, axis):
    step = ahead(value, axis) - value
    farther = jnp.where(courant >= 0.0, behind(step, axis), ahead(step, axis))
    flux = courant * value + first * step + second * farther
    return value - flux + behind(flux, axis)


def sweep_back(value, courant, first, second, axis):
    step = ahead(value, axis) - value
    reach = second * step
    forward = jnp.where(courant >= 0.0, reach, 0.0)
    total = first * step + ahead(forward, axis) + behind(reach - forward, axis)
    return value + courant * step + behind(total, axis) - total


def slopes(courant):
    c_minus = jnp.minimum(courant, 0.0)
    size = jnp.abs(courant)
    slope = 0.5 * size * (1.0 - size)
    return c_minus, c_minus + slope, slope


def window(groups, own, edges, outs, scratch):
    width, together = (ROWS + LANES, 1)
    ck, cl, ct, mx, fl, obs, mw, cw = own
    final, grad, grad_left, grad_right = outs
    (
        q, temp, lon_code, lat_code, cx, cx_minus, cx_both, cx_slope, cy, cy_minus, cy_both, cy_slope,
        inv, elim, ratio, obs_w, mw_w, force,
    ) = scratch
    lane, col_w = (lane_ids(), col_ids(width))
    strip_of = lane // EDGE
    rim = (lane < EDGE) | (lane >= LANES - EDGE)
    count_w = width // LANES
    tracers = PAIR * len(groups)
    offset = groups[0][0]
    static_left, static_right = groups[0][3:5]

    def spread(value, which, place, k):
        north, south = edges[which]
        halo = pltpu.roll(jnp.where(strip_of == k, north[place], south(place)), (LANES - EDGE * k) % LANES, 1)
        return jnp.concatenate([value, jnp.where(rim, halo, 0.0)], axis=1)

    def squeeze(right, left):
        return jnp.where(col_w < 4, right, left)

    lane_w = lax.broadcasted_iota(jnp.int32, (COLS, width), 1)
    last = lax.axis_index("lat") == lax.axis_size("lat") - 1
    pole = (lane_w == ROWS - 1) & last
    carry = [None] * 4
    for level in range(LEVELS):
        def blocks(field, k):
            own_block = spread(field[level], 0, 4 + k, level)
            right = spread(static_right[40 + 8 * k + level], 2, 4 + k, level)
            left = spread(static_left[48 + 8 * k + level], 1, 4 + k, level)
            return [own_block, right, left, squeeze(right, left)]

        for k, value in enumerate(blocks(cl, 0)):
            cx[level, k] = value
            cx_minus[level, k], cx_both[level, k], cx_slope[level, k] = slopes(value)
        for k, value in enumerate(blocks(ct, 1)):
            value = jnp.where(pole, 0.0, value)
            cy[level, k] = value
            cy_minus[level, k], cy_both[level, k], cy_slope[level, k] = slopes(value)
        for k, value in enumerate(blocks(mx, 2)):
            coupling = value if level < LEVELS - 1 else jnp.zeros_like(value)
            pivot = 1.0 + coupling
            if level > 0:
                above, above_ratio = carry[k]
                pivot = pivot + above - above * above_ratio
            inverse = 1.0 / pivot
            inv[level, k] = inverse
            ratio[level, k] = coupling * inverse
            elim[level, k] = above * inverse if level > 0 else jnp.zeros_like(value)
            carry[k] = (coupling, coupling * inverse)

    for substep in range(SUBSTEPS):
        for tracer in range(tracers):
            k = substep * TRACERS + offset + tracer
            obs_w[substep * tracers + tracer] = spread(obs[k], 0, 23 + k // 8, k % 8)
    for tracer in range(tracers):
        mw_w[tracer] = spread(mw[offset + tracer], 0, 25, offset + tracer)

    def put_codes(substep, row, blocks, lat_blocks):
        for k, value in enumerate(blocks):
            lon_code[substep, row, k] = value - jnp.where(value >= 6.0, 6.0, jnp.where(value >= 3.0, 3.0, 0.0))
        for k, value in enumerate(lat_blocks):
            lat_code[substep, row, k] = value

    for first, from_left, from_right, _, _ in groups:
        @pl.loop(0, PAIR)
        def _(within):
            for level in range(LEVELS):
                part = within * LEVELS + level
                row = (first - offset) * LEVELS + part
                whole = first * LEVELS + part
                place = first + within
                q[row, 0] = spread(ck[whole], 0, place, level)
                q[row, 1] = spread(from_right[part], 2, place, level)
                q[row, 2] = spread(from_left[part], 1, place, level)

                def tail(value, which, s):
                    return spread(value, which, 7 + s * TRACERS + place, level)

                mine = [tail(fl[s * STATE + whole].astype(jnp.float32), 0, s) for s in range(SUBSTEPS)]
                l_a, l_b = (from_left[HALF + part], from_left[2 * HALF + part])
                r_a = from_right[HALF + part]
                r_b = from_right[2 * HALF + within * 4 + level % 4]
                if level >= 4:
                    r_b = pltpu.roll(r_b, 4, 0)
                one = [mine[0], tail(r_a, 2, 0), tail(l_a, 1, 0)]
                put_codes(0, row, one, one)
                two = [mine[1], tail(r_b, 2, 1), tail(l_b, 1, 1)]
                put_codes(1, row, two, [mine[1], squeeze(two[1], two[2])])
                three = [
                    mine[2], squeeze(tail(pltpu.roll(r_a, 2, 0), 2, 2), tail(pltpu.roll(l_b, 5, 0), 1, 2))
                ]
                put_codes(2, row, three, three)
                four = [mine[3], tail(pltpu.roll(l_a, 7, 0), 1, 3)]
                put_codes(3, row, four, [mine[3]])

    def ring(slots, read):
        return jnp.concatenate([read(k) for k in slots], axis=0)

    def lon_sweep(substep, row, level, slots, pieces, back):
        code_slots = slots if len(slots) == 3 else (0, 1)
        out = []
        for chunk in range(len(pieces)):
            at = slice(chunk * LANES, (chunk + 1) * LANES)
            value = jnp.concatenate(pieces[chunk], axis=0)
            code = ring(code_slots, lambda k: lon_code[substep, row, k, :, at])
            c, c_minus, c_both, slope = [ring(slots, lambda k: f[level, k, :, at]) for f in (cx, cx_minus, cx_both, cx_slope)]
            first, second = weights(code, 1.0, 2.0, c_minus, c_both, slope)
            value = (sweep_back if back else sweep)(value, c, first, second, 0)
            out.append([value[n * COLS : (n + 1) * COLS] for n in range(len(slots))])
        return out

    def lat_weights(substep, row, level, code_slot, slot):
        return weights(
            lat_code[substep, row, code_slot], 3.0, 6.0, cy_minus[level, slot], cy_both[level, slot], cy_slope[level, slot]
        )

    def forward(substep, slots, out_slots):
        @pl.loop(0, tracers // together)
        def _(batch):
            members = [batch * together + n for n in range(together)]
            above = {}
            for level in range(LEVELS):
                for n, tracer in enumerate(members):
                    row = tracer * LEVELS + level
                    pieces = [
                        [q[row, k, :, chunk * LANES : (chunk + 1) * LANES] for k in slots] for chunk in range(count_w)
                    ]
                    pieces = lon_sweep(substep, row, level, slots, pieces, False)
                    blocks = {k: jnp.concatenate([piece[m] for piece in pieces], axis=1) for m, k in enumerate(slots)}
                    if substep == 1:
                        blocks[3] = squeeze(blocks[1], blocks[2])
                    for slot in out_slots:
                        code_slot = 1 if slot == 3 else slot
                        first, second = lat_weights(substep, row, level, code_slot, slot)
                        value = sweep(blocks[slot], cy[level, slot], first, second, 1)
                        value = value * inv[level, slot]
                        if level > 0:
                            value = value + elim[level, slot] * above[n, slot]
                        above[n, slot] = value
                        temp[row, slot] = value
            column = {}
            for level in range(LEVELS - 1, -1, -1):
                for n, tracer in enumerate(members):
                    row = tracer * LEVELS + level
                    for slot in out_slots:
                        value = above[n, slot]
                        if level < LEVELS - 1:
                            value = temp[row, slot] + ratio[level, slot] * value
                            above[n, slot] = value
                        if slot == 0:
                            part = cw[level] * value
                            column[n] = part if level == LEVELS - 1 else column[n] + part
                        if substep == SUBSTEPS - 1:
                            final[row] = value[:, :ROWS]
                        else:
                            q[row, slot] = value
            for n, tracer in enumerate(members):
                at = substep * tracers + tracer
                force[at] = mw_w[tracer] * (column[n] - obs_w[at])

    def backward(substep, slots, out_slots):
        @pl.loop(0, tracers // together)
        def _(batch):
            members = [batch * together + n for n in range(together)]
            above = {}
            for level in range(LEVELS):
                for n, tracer in enumerate(members):
                    row = tracer * LEVELS + level
                    for slot in slots:
                        if slot == 0:
                            value = cw[level] * force[substep * tracers + tracer]
                            if substep < SUBSTEPS - 1:
                                value = value + q[row, slot]
                        else:
                            value = q[row, slot]
                        value = value * inv[level, slot]
                        if level > 0:
                            value = value + elim[level, slot] * above[n, slot]
                        above[n, slot] = value
                        temp[row, slot] = value
            below = {}
            for level in range(LEVELS - 1, -1, -1):
                for n, tracer in enumerate(members):
                    row = tracer * LEVELS + level
                    blocks = {}
                    for slot in slots:
                        code_slot = 1 if slot == 3 else slot
                        value = temp[row, slot]
                        if level < LEVELS - 1:
                            value = value + ratio[level, slot] * below[n, slot]
                        below[n, slot] = value
                        first, second = lat_weights(substep, row, level, code_slot, slot)
                        blocks[slot] = sweep_back(value, cy[level, slot], first, second, 1)
                    if substep == SUBSTEPS - 1:
                        blocks[3] = jnp.zeros_like(blocks[0])
                    if substep == 1:
                        blocks[1] = jnp.where(col_w < 4, blocks[3], 0.0)
                        blocks[2] = jnp.where(col_w < 4, 0.0, blocks[3])
                    pieces = [
                        [blocks[k][:, chunk * LANES : (chunk + 1) * LANES] for k in out_slots] for chunk in range(count_w if substep else 2)
                    ]
                    pieces = lon_sweep(substep, row, level, out_slots, pieces, True)
                    for chunk in range(len(pieces)):
                        at = slice(chunk * LANES, (chunk + 1) * LANES)
                        for m, k in enumerate(out_slots):
                            if substep == 0:
                                (grad, grad_right, grad_left)[k][row, :, at] = pieces[chunk][m]
                            else:
                                q[row, k, :, at] = pieces[chunk][m]

    three, two = ((0, 1, 2), (0, 3))
    forward(0, three, three)
    forward(1, three, two)
    forward(2, two, two)
    forward(3, two, (0,))
    backward(3, (0,), two)
    backward(2, two, two)
    backward(1, two, three)
    backward(0, three, three)


def halves(half, *refs):
    own, (left_a, right_a), (north, south, corner_l, corner_r) = (refs[:8], refs[8:10], refs[10:14])
    refs = refs[14:]
    edges = (
        (north, lambda k: south[k]),
        (corner_l, lambda k: corner_l[CORNER + k]),
        (corner_r, lambda k: corner_r[CORNER + k]),
    )
    if half == 0:
        outs, scratch = (refs[:4], refs[4:])
        groups = [(0, left_a, right_a, left_a, right_a)]
    else:
        left_b, right_b, before = refs[:3]
        final, outs, scratch = (refs[3], refs[4:7], refs[7:])
        final[0:HALF] = before[...]
        outs = (final.at[HALF:STATE],) + tuple(outs)
        groups = [(PAIR, left_b, right_b, left_a, right_a)]
    window(groups, own, edges, outs, scratch)


def finish(*refs):
    out = refs[6]
    for half in range(2):
        own, right, left = refs[3 * half : 3 * half + 3]

        @pl.loop(0, HALF)
        def _(row):
            out[half * HALF + row] = own[row] + right[row] + left[row]


def spec(count, space=pltpu.VMEM):
    return [pl.BlockSpec(memory_space=space)] * count


def scratch_for(width, tracers):
    rows = tracers * LEVELS
    sizes = [(rows, 4)] * 2 + [(SUBSTEPS, rows, 3)] * 2 + [(LEVELS, 4)] * 11 + [(SUBSTEPS * tracers,), (tracers,), (SUBSTEPS * tracers,)]
    return [pltpu.VMEM(size + (COLS, width), jnp.float32) for size in sizes]


def shards(
    checkpoint, courant_lon, courant_lat, mixing, limiter_flags, column_weights, observations, misfit_weight
):
    def block(rows, lanes=ROWS):
        return jax.ShapeDtypeStruct((rows, COLS, lanes), jnp.float32)

    def call(kernel, name, outs, in_specs, operands, scratch=(), limit=LIMIT):
        return pl.pallas_call(
            kernel,
            out_shape=tuple(outs),
            in_specs=in_specs,
            out_specs=tuple(spec(len(outs))),
            scratch_shapes=list(scratch),
            compiler_params=pltpu.CompilerParams(vmem_limit_bytes=limit),
            name=name,
        )(*operands)

    lat, lon = (lax.axis_size("lat"), lax.axis_size("lon"))
    east = [(i, (i + 1) % lon) for i in range(lon)]
    west = [(j, i) for i, j in east]
    up = [(i, i + 1) for i in range(lat - 1)]
    down = [(j, i) for i, j in up]
    own = (
        checkpoint.reshape((STATE, COLS, ROWS)),
        courant_lon,
        courant_lat,
        mixing,
        limiter_flags.reshape((SUBSTEPS * STATE, COLS, ROWS)),
        observations.reshape((SUBSTEPS * TRACERS, COLS, ROWS)),
        misfit_weight,
    )
    hbm = spec(1, pltpu.HBM)
    held = [pltpu.VMEM(value.shape, value.dtype) for value in own]
    to_north, to_south = call(
        pack_lat, "pack_lat", [block(26, LANES)] * 2, hbm * 7, own, held + [pltpu.SemaphoreType.DMA((7,))], limit=PACK_LIMIT
    )
    right_a, right_b, left_a, left_b = call(
        pack_lon, "pack_lon", [block(72), block(48), block(64), block(40)], hbm * 6, own[:5] + (to_north,),
        held[:5] + [pltpu.SemaphoreType.DMA((5,))], limit=PACK_LIMIT,
    )
    south = lax.ppermute(to_north, "lat", up)
    north = lax.ppermute(to_south, "lat", down)
    from_left_a = lax.ppermute(right_a, "lon", east)
    from_right_a = lax.ppermute(left_a, "lon", west)
    (corner,) = call(join, "join", [block(2 * CORNER, LANES)], spec(9), own + (north, south))
    corner_l = lax.ppermute(corner, "lon", east)
    corner_r = lax.ppermute(corner, "lon", west)
    from_left_a, from_right_a, corner_l, corner_r, right_b, left_b = lax.optimization_barrier(
        (from_left_a, from_right_a, corner_l, corner_r, right_b, left_b)
    )
    from_left_b = lax.ppermute(right_b, "lon", east)
    from_right_b = lax.ppermute(left_b, "lon", west)
    smem = spec(1, pltpu.SMEM)
    operands = own + (column_weights, from_left_a, from_right_a, north, south, corner_l, corner_r)
    final_a, grad_a, gl_a, gr_a = call(
        functools.partial(halves, 0), "window_first", [block(HALF)] * 4, spec(7) + smem + spec(6), operands,
        scratch_for(ROWS + LANES, PAIR),
    )
    from_right_1 = lax.ppermute(gl_a, "lon", west)
    from_left_1 = lax.ppermute(gr_a, "lon", east)
    final, grad_b, gl_b, gr_b = call(
        functools.partial(halves, 1), "window_second", [block(STATE)] + [block(HALF)] * 3, spec(7) + smem + spec(9),
        operands + (from_left_b, from_right_b, final_a), scratch_for(ROWS + LANES, PAIR),
    )
    from_right_2 = lax.ppermute(gl_b, "lon", west)
    from_left_2 = lax.ppermute(gr_b, "lon", east)
    (grad,) = call(
        finish, "finish", [block(STATE)], spec(6),
        (grad_a, from_right_1, from_left_1, grad_b, from_right_2, from_left_2),
    )
    return (final.reshape(checkpoint.shape), grad.reshape(checkpoint.shape))


def solution(mesh):
    return jax.shard_map(
        shards,
        mesh=mesh,
        in_specs=(
            P(None, None, "lon", "lat"),
            P(None, "lon", "lat"),
            P(None, "lon", "lat"),
            P(None, "lon", "lat"),
            P(None, None, None, "lon", "lat"),
            P(),
            P(None, None, "lon", "lat"),
            P(None, "lon", "lat"),
        ),
        out_specs=(P(None, None, "lon", "lat"), P(None, None, "lon", "lat")),
        check_vma=False,
    )
```

```python
import functools

import jax
import jax.numpy as jnp
from jax import lax
from jax.experimental import pallas as pl
from jax.experimental.pallas import tpu as pltpu
from jax.sharding import PartitionSpec as P

TRACERS, LEVELS, SUBSTEPS = 4, 8, 4
PAIR = 2
COLS, ROWS, EDGE, LANES = 8, 256, 16, 128
STATE = TRACERS * LEVELS
HALF = PAIR * LEVELS
LIMIT = 24 * 1024 * 1024
PACK_LIMIT = 60 * 1024 * 1024
CORNER = 23


def lane_ids():
    return lax.broadcasted_iota(jnp.int32, (COLS, LANES), 1)


def col_ids(lanes=LANES):
    return lax.broadcasted_iota(jnp.int32, (COLS, lanes), 0)


def fetch(hbm, own, sems):
    copies = [pltpu.make_async_copy(source, target, sems.at[k]) for k, (source, target) in enumerate(zip(hbm, own))]
    for copy in copies:
        copy.start()
    for copy in copies:
        copy.wait()


def pack(*refs):
    hbm, (right_a, right_b, left_a, left_b, to_north, to_south), own, sems = (refs[:7], refs[7:13], refs[13:20], refs[20])
    fetch(hbm, own, sems)
    ck, cl, ct, mx, fl, obs, mw = own
    lane = lane_ids()
    col = col_ids(ROWS)
    for half, (to_right, to_left) in enumerate(((right_a, left_a), (right_b, left_b))):
        to_right[0:HALF] = ck[half * HALF : (half + 1) * HALF]
        to_left[0:HALF] = ck[half * HALF : (half + 1) * HALF]

        @pl.loop(0, PAIR)
        def _(tracer):
            for level in range(LEVELS):
                row = tracer * LEVELS + level
                one, two, three, four = [
                    fl[s * STATE + half * HALF + row].astype(jnp.float32) for s in range(SUBSTEPS)
                ]
                to_right[HALF + row] = jnp.where(col >= 1, one, pltpu.roll(four, 1, 0))
                to_right[2 * HALF + row] = jnp.where(col >= 3, two, pltpu.roll(three, 3, 0))
                to_left[HALF + row] = jnp.where(col < 6, one, pltpu.roll(three, 6, 0))
                if level < 4:
                    other = fl[STATE + half * HALF + row + 4].astype(jnp.float32)
                    to_left[2 * HALF + tracer * 4 + level] = jnp.where(col < 4, two, pltpu.roll(other, 4, 0))

    for k, field in enumerate((cl, ct, mx)):
        right_a[3 * HALF + 8 * k : 3 * HALF + 8 * k + 8] = field[...]
        left_a[40 + 8 * k : 48 + 8 * k] = field[...]

    def strips(place, read, count):
        north = jnp.zeros((COLS, LANES), jnp.float32)
        south = north
        for k in range(count):
            whole = read(k)
            here = lane // EDGE
            north = jnp.where(here == (k + 7) % 8, pltpu.roll(whole[:, LANES:], EDGE * k, 1), north)
            south = jnp.where(here == k, pltpu.roll(whole[:, :LANES], EDGE * k, 1), south)
        to_north[place] = north
        to_south[place] = south

    @pl.loop(0, TRACERS)
    def _(tracer):
        strips(tracer, lambda k: ck[tracer * LEVELS + k], LEVELS)

    for place, field in ((4, cl), (5, ct), (6, mx)):
        strips(place, lambda k, field=field: field[k], LEVELS)

    @pl.loop(0, SUBSTEPS * TRACERS)
    def _(block):
        strips(7 + block, lambda k: fl[block * LEVELS + k].astype(jnp.float32), LEVELS)

    for half in range(2):
        strips(23 + half, lambda k, half=half: obs[half * 8 + k], 8)
    strips(25, lambda k: mw[k], TRACERS)


def join(*refs):
    north, south, out = (refs[7], refs[8], refs[9])
    out[0:CORNER] = north[0:CORNER]
    out[CORNER : 2 * CORNER] = south[0:CORNER]


def behind(value, axis):
    return pltpu.roll(value, 1, axis)


def ahead(value, axis):
    return pltpu.roll(value, value.shape[axis] - 1, axis)


def weights(branch, low, high, c_minus, c_both, slope):
    first = jnp.where(branch >= high, c_minus, jnp.where(branch >= low, c_both, c_minus))
    return first, jnp.where(branch >= high, slope, 0.0)


def sweep(value, courant, first, second, axis):
    step = ahead(value, axis) - value
    farther = jnp.where(courant >= 0.0, behind(step, axis), ahead(step, axis))
    flux = courant * value + first * step + second * farther
    return value - flux + behind(flux, axis)


def sweep_back(value, courant, first, second, axis):
    step = ahead(value, axis) - value
    reach = second * step
    forward = jnp.where(courant >= 0.0, reach, 0.0)
    total = first * step + ahead(forward, axis) + behind(reach - forward, axis)
    return value + courant * step + behind(total, axis) - total


def slopes(courant):
    c_minus = jnp.minimum(courant, 0.0)
    size = jnp.abs(courant)
    slope = 0.5 * size * (1.0 - size)
    return c_minus, c_minus + slope, slope


def window(groups, own, edges, outs, scratch):
    width, together = (ROWS + LANES, 1)
    ck, cl, ct, mx, fl, obs, mw, cw = own
    final, grad, grad_left, grad_right = outs
    (
        q, temp, lon_code, lat_code, cx, cx_minus, cx_both, cx_slope, cy, cy_minus, cy_both, cy_slope,
        inv, elim, ratio, obs_w, mw_w, force,
    ) = scratch
    lane, col_w = (lane_ids(), col_ids(width))
    strip_of = lane // EDGE
    rim = (lane < EDGE) | (lane >= LANES - EDGE)
    count_w = width // LANES
    tracers = PAIR * len(groups)
    offset = groups[0][0]
    static_left, static_right = groups[0][3:5]

    def spread(value, which, place, k):
        north, south = edges[which]
        halo = pltpu.roll(jnp.where(strip_of == k, north[place], south(place)), (LANES - EDGE * k) % LANES, 1)
        return jnp.concatenate([value, jnp.where(rim, halo, 0.0)], axis=1)

    def squeeze(right, left):
        return jnp.where(col_w < 4, right, left)

    lane_w = lax.broadcasted_iota(jnp.int32, (COLS, width), 1)
    last = lax.axis_index("lat") == lax.axis_size("lat") - 1
    pole = (lane_w == ROWS - 1) & last
    carry = [None] * 4
    for level in range(LEVELS):
        def blocks(field, k):
            own_block = spread(field[level], 0, 4 + k, level)
            right = spread(static_right[40 + 8 * k + level], 2, 4 + k, level)
            left = spread(static_left[48 + 8 * k + level], 1, 4 + k, level)
            return [own_block, right, left, squeeze(right, left)]

        for k, value in enumerate(blocks(cl, 0)):
            cx[level, k] = value
            cx_minus[level, k], cx_both[level, k], cx_slope[level, k] = slopes(value)
        for k, value in enumerate(blocks(ct, 1)):
            value = jnp.where(pole, 0.0, value)
            cy[level, k] = value
            cy_minus[level, k], cy_both[level, k], cy_slope[level, k] = slopes(value)
        for k, value in enumerate(blocks(mx, 2)):
            coupling = value if level < LEVELS - 1 else jnp.zeros_like(value)
            pivot = 1.0 + coupling
            if level > 0:
                above, above_ratio = carry[k]
                pivot = pivot + above - above * above_ratio
            inverse = 1.0 / pivot
            inv[level, k] = inverse
            ratio[level, k] = coupling * inverse
            elim[level, k] = above * inverse if level > 0 else jnp.zeros_like(value)
            carry[k] = (coupling, coupling * inverse)

    for substep in range(SUBSTEPS):
        for tracer in range(tracers):
            k = substep * TRACERS + offset + tracer
            obs_w[substep * tracers + tracer] = spread(obs[k], 0, 23 + k // 8, k % 8)
    for tracer in range(tracers):
        mw_w[tracer] = spread(mw[offset + tracer], 0, 25, offset + tracer)

    def put_codes(substep, row, blocks, lat_blocks):
        for k, value in enumerate(blocks):
            lon_code[substep, row, k] = value - jnp.where(value >= 6.0, 6.0, jnp.where(value >= 3.0, 3.0, 0.0))
        for k, value in enumerate(lat_blocks):
            lat_code[substep, row, k] = value

    for first, from_left, from_right, _, _ in groups:
        @pl.loop(0, PAIR)
        def _(within):
            for level in range(LEVELS):
                part = within * LEVELS + level
                row = (first - offset) * LEVELS + part
                whole = first * LEVELS + part
                place = first + within
                q[row, 0] = spread(ck[whole], 0, place, level)
                q[row, 1] = spread(from_right[part], 2, place, level)
                q[row, 2] = spread(from_left[part], 1, place, level)

                def tail(value, which, s):
                    return spread(value, which, 7 + s * TRACERS + place, level)

                mine = [tail(fl[s * STATE + whole].astype(jnp.float32), 0, s) for s in range(SUBSTEPS)]
                l_a, l_b = (from_left[HALF + part], from_left[2 * HALF + part])
                r_a = from_right[HALF + part]
                r_b = from_right[2 * HALF + within * 4 + level % 4]
                if level >= 4:
                    r_b = pltpu.roll(r_b, 4, 0)
                one = [mine[0], tail(r_a, 2, 0), tail(l_a, 1, 0)]
                put_codes(0, row, one, one)
                two = [mine[1], tail(r_b, 2, 1), tail(l_b, 1, 1)]
                put_codes(1, row, two, [mine[1], squeeze(two[1], two[2])])
                three = [
                    mine[2], squeeze(tail(pltpu.roll(r_a, 2, 0), 2, 2), tail(pltpu.roll(l_b, 5, 0), 1, 2))
                ]
                put_codes(2, row, three, three)
                four = [mine[3], tail(pltpu.roll(l_a, 7, 0), 1, 3)]
                put_codes(3, row, four, [mine[3]])

    def ring(slots, read):
        return jnp.concatenate([read(k) for k in slots], axis=0)

    def lon_sweep(substep, row, level, slots, pieces, back):
        code_slots = slots if len(slots) == 3 else (0, 1)
        at = slice(0, len(pieces) * LANES)
        value = jnp.concatenate([jnp.concatenate(piece, axis=0) for piece in pieces], axis=1)
        code = ring(code_slots, lambda k: lon_code[substep, row, k, :, at])
        c, c_minus, c_both, slope = [ring(slots, lambda k: f[level, k, :, at]) for f in (cx, cx_minus, cx_both, cx_slope)]
        first, second = weights(code, 1.0, 2.0, c_minus, c_both, slope)
        value = (sweep_back if back else sweep)(value, c, first, second, 0)
        return [
            [value[n * COLS : (n + 1) * COLS, chunk * LANES : (chunk + 1) * LANES] for n in range(len(slots))]
            for chunk in range(len(pieces))
        ]

    def lat_weights(substep, row, level, slots):
        code = ring(slots, lambda k: lat_code[substep, row, 1 if k == 3 else k])
        return weights(code, 3.0, 6.0, *[ring(slots, lambda k: f[level, k]) for f in (cy_minus, cy_both, cy_slope)])

    def forward(substep, slots, out_slots):
        @pl.loop(0, tracers // together)
        def _(batch):
            members = [batch * together + n for n in range(together)]
            above = {}
            for level in range(LEVELS):
                for n, tracer in enumerate(members):
                    row = tracer * LEVELS + level
                    pieces = [
                        [q[row, k, :, chunk * LANES : (chunk + 1) * LANES] for k in slots] for chunk in range(count_w)
                    ]
                    pieces = lon_sweep(substep, row, level, slots, pieces, False)
                    blocks = {k: jnp.concatenate([piece[m] for piece in pieces], axis=1) for m, k in enumerate(slots)}
                    if substep == 1:
                        blocks[3] = squeeze(blocks[1], blocks[2])
                    value = jnp.concatenate([blocks[slot] for slot in out_slots], axis=0)
                    first, second = lat_weights(substep, row, level, out_slots)
                    value = sweep(value, ring(out_slots, lambda k: cy[level, k]), first, second, 1)
                    for m, slot in enumerate(out_slots):
                        part = value[m * COLS : (m + 1) * COLS] * inv[level, slot]
                        if level > 0:
                            part = part + elim[level, slot] * above[n, slot]
                        above[n, slot] = part
                        temp[row, slot] = part
            column = {}
            for level in range(LEVELS - 1, -1, -1):
                for n, tracer in enumerate(members):
                    row = tracer * LEVELS + level
                    for slot in out_slots:
                        value = above[n, slot]
                        if level < LEVELS - 1:
                            value = temp[row, slot] + ratio[level, slot] * value
                            above[n, slot] = value
                        if slot == 0:
                            part = cw[level] * value
                            column[n] = part if level == LEVELS - 1 else column[n] + part
                        if substep == SUBSTEPS - 1:
                            final[row] = value[:, :ROWS]
                        else:
                            q[row, slot] = value
            for n, tracer in enumerate(members):
                at = substep * tracers + tracer
                force[at] = mw_w[tracer] * (column[n] - obs_w[at])

    def backward(substep, slots, out_slots):
        @pl.loop(0, tracers // together)
        def _(batch):
            members = [batch * together + n for n in range(together)]
            above = {}
            for level in range(LEVELS):
                for n, tracer in enumerate(members):
                    row = tracer * LEVELS + level
                    for slot in slots:
                        if slot == 0:
                            value = cw[level] * force[substep * tracers + tracer]
                            if substep < SUBSTEPS - 1:
                                value = value + q[row, slot]
                        else:
                            value = q[row, slot]
                        value = value * inv[level, slot]
                        if level > 0:
                            value = value + elim[level, slot] * above[n, slot]
                        above[n, slot] = value
                        temp[row, slot] = value
            below = {}
            for level in range(LEVELS - 1, -1, -1):
                for n, tracer in enumerate(members):
                    row = tracer * LEVELS + level
                    blocks = {}
                    for slot in slots:
                        value = temp[row, slot]
                        if level < LEVELS - 1:
                            value = value + ratio[level, slot] * below[n, slot]
                        below[n, slot] = value
                    first, second = lat_weights(substep, row, level, slots)
                    value = jnp.concatenate([below[n, slot] for slot in slots], axis=0)
                    value = sweep_back(value, ring(slots, lambda k: cy[level, k]), first, second, 1)
                    for m, slot in enumerate(slots):
                        blocks[slot] = value[m * COLS : (m + 1) * COLS]
                    if substep == SUBSTEPS - 1:
                        blocks[3] = jnp.zeros_like(blocks[0])
                    if substep == 1:
                        blocks[1] = jnp.where(col_w < 4, blocks[3], 0.0)
                        blocks[2] = jnp.where(col_w < 4, 0.0, blocks[3])
                    pieces = [
                        [blocks[k][:, chunk * LANES : (chunk + 1) * LANES] for k in out_slots] for chunk in range(count_w if substep else 2)
                    ]
                    pieces = lon_sweep(substep, row, level, out_slots, pieces, True)
                    for chunk in range(len(pieces)):
                        at = slice(chunk * LANES, (chunk + 1) * LANES)
                        for m, k in enumerate(out_slots):
                            if substep == 0:
                                (grad, grad_right, grad_left)[k][row, :, at] = pieces[chunk][m]
                            else:
                                q[row, k, :, at] = pieces[chunk][m]

    three, two = ((0, 1, 2), (0, 3))
    forward(0, three, three)
    forward(1, three, two)
    forward(2, two, two)
    forward(3, two, (0,))
    backward(3, (0,), two)
    backward(2, two, two)
    backward(1, two, three)
    backward(0, three, three)


def halves(half, *refs):
    own, (left_a, right_a), (north, south, corner_l, corner_r) = (refs[:8], refs[8:10], refs[10:14])
    refs = refs[14:]
    edges = (
        (north, lambda k: south[k]),
        (corner_l, lambda k: corner_l[CORNER + k]),
        (corner_r, lambda k: corner_r[CORNER + k]),
    )
    if half == 0:
        outs, scratch = (refs[:4], refs[4:])
        groups = [(0, left_a, right_a, left_a, right_a)]
    else:
        left_b, right_b, before = refs[:3]
        final, outs, scratch = (refs[3], refs[4:7], refs[7:])
        final[0:HALF] = before[...]
        outs = (final.at[HALF:STATE],) + tuple(outs)
        groups = [(PAIR, left_b, right_b, left_a, right_a)]
    window(groups, own, edges, outs, scratch)


def finish(*refs):
    out = refs[6]
    for half in range(2):
        own, right, left = refs[3 * half : 3 * half + 3]

        @pl.loop(0, HALF)
        def _(row):
            out[half * HALF + row] = own[row] + right[row] + left[row]


def spec(count, space=pltpu.VMEM):
    return [pl.BlockSpec(memory_space=space)] * count


def scratch_for(width, tracers):
    rows = tracers * LEVELS
    sizes = [(rows, 4)] * 2 + [(SUBSTEPS, rows, 3)] * 2 + [(LEVELS, 4)] * 11 + [(SUBSTEPS * tracers,), (tracers,), (SUBSTEPS * tracers,)]
    return [pltpu.VMEM(size + (COLS, width), jnp.float32) for size in sizes]


def shards(
    checkpoint, courant_lon, courant_lat, mixing, limiter_flags, column_weights, observations, misfit_weight
):
    def block(rows, lanes=ROWS):
        return jax.ShapeDtypeStruct((rows, COLS, lanes), jnp.float32)

    def call(kernel, name, outs, in_specs, operands, scratch=(), limit=LIMIT):
        return pl.pallas_call(
            kernel,
            out_shape=tuple(outs),
            in_specs=in_specs,
            out_specs=tuple(spec(len(outs))),
            scratch_shapes=list(scratch),
            compiler_params=pltpu.CompilerParams(vmem_limit_bytes=limit),
            name=name,
        )(*operands)

    lat, lon = (lax.axis_size("lat"), lax.axis_size("lon"))
    east = [(i, (i + 1) % lon) for i in range(lon)]
    west = [(j, i) for i, j in east]
    up = [(i, i + 1) for i in range(lat - 1)]
    down = [(j, i) for i, j in up]
    own = (
        checkpoint.reshape((STATE, COLS, ROWS)),
        courant_lon,
        courant_lat,
        mixing,
        limiter_flags.reshape((SUBSTEPS * STATE, COLS, ROWS)),
        observations.reshape((SUBSTEPS * TRACERS, COLS, ROWS)),
        misfit_weight,
    )
    hbm = spec(1, pltpu.HBM)
    held = [pltpu.VMEM(value.shape, value.dtype) for value in own]
    right_a, right_b, left_a, left_b, to_north, to_south = call(
        pack,
        "pack",
        [block(72), block(48), block(64), block(40), block(26, LANES), block(26, LANES)],
        hbm * 7,
        own,
        held + [pltpu.SemaphoreType.DMA((7,))],
        limit=PACK_LIMIT,
    )
    south = lax.ppermute(to_north, "lat", up)
    north = lax.ppermute(to_south, "lat", down)
    from_left_a = lax.ppermute(right_a, "lon", east)
    from_right_a = lax.ppermute(left_a, "lon", west)
    (corner,) = call(join, "join", [block(2 * CORNER, LANES)], spec(9), own + (north, south))
    corner_l = lax.ppermute(corner, "lon", east)
    corner_r = lax.ppermute(corner, "lon", west)
    from_left_a, from_right_a, corner_l, corner_r, right_b, left_b = lax.optimization_barrier(
        (from_left_a, from_right_a, corner_l, corner_r, right_b, left_b)
    )
    from_left_b = lax.ppermute(right_b, "lon", east)
    from_right_b = lax.ppermute(left_b, "lon", west)
    smem = spec(1, pltpu.SMEM)
    operands = own + (column_weights, from_left_a, from_right_a, north, south, corner_l, corner_r)
    final_a, grad_a, gl_a, gr_a = call(
        functools.partial(halves, 0), "window_first", [block(HALF)] * 4, spec(7) + smem + spec(6), operands,
        scratch_for(ROWS + LANES, PAIR),
    )
    from_right_1 = lax.ppermute(gl_a, "lon", west)
    from_left_1 = lax.ppermute(gr_a, "lon", east)
    final, grad_b, gl_b, gr_b = call(
        functools.partial(halves, 1), "window_second", [block(STATE)] + [block(HALF)] * 3, spec(7) + smem + spec(9),
        operands + (from_left_b, from_right_b, final_a), scratch_for(ROWS + LANES, PAIR),
    )
    from_right_2 = lax.ppermute(gl_b, "lon", west)
    from_left_2 = lax.ppermute(gr_b, "lon", east)
    (grad,) = call(
        finish, "finish", [block(STATE)], spec(6),
        (grad_a, from_right_1, from_left_1, grad_b, from_right_2, from_left_2),
    )
    return (final.reshape(checkpoint.shape), grad.reshape(checkpoint.shape))


def solution(mesh):
    return jax.shard_map(
        shards,
        mesh=mesh,
        in_specs=(
            P(None, None, "lon", "lat"),
            P(None, "lon", "lat"),
            P(None, "lon", "lat"),
            P(None, "lon", "lat"),
            P(None, None, None, "lon", "lat"),
            P(),
            P(None, None, "lon", "lat"),
            P(None, "lon", "lat"),
        ),
        out_specs=(P(None, None, "lon", "lat"), P(None, None, "lon", "lat")),
        check_vma=False,
    )
```

```python
import functools

import jax
import jax.numpy as jnp
from jax import lax
from jax.experimental import pallas as pl
from jax.experimental.pallas import tpu as pltpu
from jax.sharding import PartitionSpec as P

TRACERS, LEVELS, SUBSTEPS = 4, 8, 4
PAIR = 2
COLS, ROWS, EDGE, LANES = 8, 256, 16, 128
STATE = TRACERS * LEVELS
HALF = PAIR * LEVELS
LIMIT = 24 * 1024 * 1024
PACK_LIMIT = 60 * 1024 * 1024
CORNER = 23


def lane_ids():
    return lax.broadcasted_iota(jnp.int32, (COLS, LANES), 1)


def col_ids(lanes=LANES):
    return lax.broadcasted_iota(jnp.int32, (COLS, lanes), 0)


def fetch(hbm, own, sems):
    copies = [pltpu.make_async_copy(source, target, sems.at[k]) for k, (source, target) in enumerate(zip(hbm, own))]
    for copy in copies:
        copy.start()
    for copy in copies:
        copy.wait()


def pack(*refs):
    hbm, (right_a, right_b, left_a, left_b, to_north, to_south), own, sems = (refs[:7], refs[7:13], refs[13:20], refs[20])
    fetch(hbm, own, sems)
    ck, cl, ct, mx, fl, obs, mw = own
    lane = lane_ids()
    col = col_ids(ROWS)
    for half, (to_right, to_left) in enumerate(((right_a, left_a), (right_b, left_b))):
        to_right[0:HALF] = ck[half * HALF : (half + 1) * HALF]
        to_left[0:HALF] = ck[half * HALF : (half + 1) * HALF]

        @pl.loop(0, PAIR)
        def _(tracer):
            for level in range(LEVELS):
                row = tracer * LEVELS + level
                one, two, three, four = [
                    fl[s * STATE + half * HALF + row].astype(jnp.float32) for s in range(SUBSTEPS)
                ]
                to_right[HALF + row] = jnp.where(col >= 1, one, pltpu.roll(four, 1, 0))
                to_right[2 * HALF + row] = jnp.where(col >= 3, two, pltpu.roll(three, 3, 0))
                to_left[HALF + row] = jnp.where(col < 6, one, pltpu.roll(three, 6, 0))
                if level < 4:
                    other = fl[STATE + half * HALF + row + 4].astype(jnp.float32)
                    to_left[2 * HALF + tracer * 4 + level] = jnp.where(col < 4, two, pltpu.roll(other, 4, 0))

    for k, field in enumerate((cl, ct, mx)):
        right_a[3 * HALF + 8 * k : 3 * HALF + 8 * k + 8] = field[...]
        left_a[40 + 8 * k : 48 + 8 * k] = field[...]

    def strips(place, read, count):
        north = jnp.zeros((COLS, LANES), jnp.float32)
        south = north
        for k in range(count):
            whole = read(k)
            here = lane // EDGE
            north = jnp.where(here == (k + 7) % 8, pltpu.roll(whole[:, LANES:], EDGE * k, 1), north)
            south = jnp.where(here == k, pltpu.roll(whole[:, :LANES], EDGE * k, 1), south)
        to_north[place] = north
        to_south[place] = south

    @pl.loop(0, TRACERS)
    def _(tracer):
        strips(tracer, lambda k: ck[tracer * LEVELS + k], LEVELS)

    for place, field in ((4, cl), (5, ct), (6, mx)):
        strips(place, lambda k, field=field: field[k], LEVELS)

    @pl.loop(0, SUBSTEPS * TRACERS)
    def _(block):
        strips(7 + block, lambda k: fl[block * LEVELS + k].astype(jnp.float32), LEVELS)

    for half in range(2):
        strips(23 + half, lambda k, half=half: obs[half * 8 + k], 8)
    strips(25, lambda k: mw[k], TRACERS)


def join(*refs):
    north, south, out = (refs[7], refs[8], refs[9])
    out[0:CORNER] = north[0:CORNER]
    out[CORNER : 2 * CORNER] = south[0:CORNER]


def behind(value, axis):
    return pltpu.roll(value, 1, axis)


def ahead(value, axis):
    return pltpu.roll(value, value.shape[axis] - 1, axis)


def weights(branch, low, high, c_minus, c_both, slope):
    first = jnp.where(branch >= high, c_minus, jnp.where(branch >= low, c_both, c_minus))
    return first, jnp.where(branch >= high, slope, 0.0)


def sweep(value, courant, first, second, axis):
    step = ahead(value, axis) - value
    farther = jnp.where(courant >= 0.0, behind(step, axis), ahead(step, axis))
    flux = courant * value + first * step + second * farther
    return value - flux + behind(flux, axis)


def sweep_back(value, courant, first, second, axis):
    step = ahead(value, axis) - value
    reach = second * step
    forward = jnp.where(courant >= 0.0, reach, 0.0)
    total = first * step + ahead(forward, axis) + behind(reach - forward, axis)
    return value + courant * step + behind(total, axis) - total


def slopes(courant):
    c_minus = jnp.minimum(courant, 0.0)
    size = jnp.abs(courant)
    slope = 0.5 * size * (1.0 - size)
    return c_minus, c_minus + slope, slope


def window(groups, own, edges, outs, scratch):
    width, together = (ROWS + LANES, 1)
    ck, cl, ct, mx, fl, obs, mw, cw = own
    final, grad, grad_left, grad_right = outs
    (
        q, temp, lon_code, lat_code, cx, cx_minus, cx_both, cx_slope, cy, cy_minus, cy_both, cy_slope,
        inv, elim, ratio, obs_w, mw_w, force,
    ) = scratch
    lane, col_w = (lane_ids(), col_ids(width))
    strip_of = lane // EDGE
    rim = (lane < EDGE) | (lane >= LANES - EDGE)
    count_w = width // LANES
    tracers = PAIR * len(groups)
    offset = groups[0][0]
    static_left, static_right = groups[0][3:5]

    def spread(value, which, place, k):
        north, south = edges[which]
        halo = pltpu.roll(jnp.where(strip_of == k, north[place], south(place)), (LANES - EDGE * k) % LANES, 1)
        return jnp.concatenate([value, jnp.where(rim, halo, 0.0)], axis=1)

    def squeeze(right, left):
        return jnp.where(col_w < 4, right, left)

    lane_w = lax.broadcasted_iota(jnp.int32, (COLS, width), 1)
    last = lax.axis_index("lat") == lax.axis_size("lat") - 1
    pole = (lane_w == ROWS - 1) & last
    carry = [None] * 4
    for level in range(LEVELS):
        def blocks(field, k):
            own_block = spread(field[level], 0, 4 + k, level)
            right = spread(static_right[40 + 8 * k + level], 2, 4 + k, level)
            left = spread(static_left[48 + 8 * k + level], 1, 4 + k, level)
            return [own_block, right, left, squeeze(right, left)]

        for k, value in enumerate(blocks(cl, 0)):
            cx[level, k] = value
            cx_minus[level, k], cx_both[level, k], cx_slope[level, k] = slopes(value)
        for k, value in enumerate(blocks(ct, 1)):
            value = jnp.where(pole, 0.0, value)
            cy[level, k] = value
            cy_minus[level, k], cy_both[level, k], cy_slope[level, k] = slopes(value)
        for k, value in enumerate(blocks(mx, 2)):
            coupling = value if level < LEVELS - 1 else jnp.zeros_like(value)
            pivot = 1.0 + coupling
            if level > 0:
                above, above_ratio = carry[k]
                pivot = pivot + above - above * above_ratio
            inverse = 1.0 / pivot
            inv[level, k] = inverse
            ratio[level, k] = coupling * inverse
            elim[level, k] = above * inverse if level > 0 else jnp.zeros_like(value)
            carry[k] = (coupling, coupling * inverse)

    for substep in range(SUBSTEPS):
        for tracer in range(tracers):
            k = substep * TRACERS + offset + tracer
            obs_w[substep * tracers + tracer] = spread(obs[k], 0, 23 + k // 8, k % 8)
    for tracer in range(tracers):
        mw_w[tracer] = spread(mw[offset + tracer], 0, 25, offset + tracer)

    def put_codes(substep, row, blocks, lat_blocks):
        for k, value in enumerate(blocks):
            lon_code[substep, row, k] = value - jnp.where(value >= 6.0, 6.0, jnp.where(value >= 3.0, 3.0, 0.0))
        for k, value in enumerate(lat_blocks):
            lat_code[substep, row, k] = value

    for first, from_left, from_right, _, _ in groups:
        @pl.loop(0, PAIR)
        def _(within):
            for level in range(LEVELS):
                part = within * LEVELS + level
                row = (first - offset) * LEVELS + part
                whole = first * LEVELS + part
                place = first + within
                q[row, 0] = spread(ck[whole], 0, place, level)
                q[row, 1] = spread(from_right[part], 2, place, level)
                q[row, 2] = spread(from_left[part], 1, place, level)

                def tail(value, which, s):
                    return spread(value, which, 7 + s * TRACERS + place, level)

                mine = [tail(fl[s * STATE + whole].astype(jnp.float32), 0, s) for s in range(SUBSTEPS)]
                l_a, l_b = (from_left[HALF + part], from_left[2 * HALF + part])
                r_a = from_right[HALF + part]
                r_b = from_right[2 * HALF + within * 4 + level % 4]
                if level >= 4:
                    r_b = pltpu.roll(r_b, 4, 0)
                one = [mine[0], tail(r_a, 2, 0), tail(l_a, 1, 0)]
                put_codes(0, row, one, one)
                two = [mine[1], tail(r_b, 2, 1), tail(l_b, 1, 1)]
                put_codes(1, row, two, [mine[1], squeeze(two[1], two[2])])
                three = [
                    mine[2], squeeze(tail(pltpu.roll(r_a, 2, 0), 2, 2), tail(pltpu.roll(l_b, 5, 0), 1, 2))
                ]
                put_codes(2, row, three, three)
                four = [mine[3], tail(pltpu.roll(l_a, 7, 0), 1, 3)]
                put_codes(3, row, four, [mine[3]])

    def ring(slots, read):
        return jnp.concatenate([read(k) for k in slots], axis=0)

    def lon_sweep(substep, row, level, slots, pieces, back):
        code_slots = slots if len(slots) == 3 else (0, 1)
        at = slice(0, len(pieces) * LANES)
        value = jnp.concatenate([jnp.concatenate(piece, axis=0) for piece in pieces], axis=1)
        code = ring(code_slots, lambda k: lon_code[substep, row, k, :, at])
        c, c_minus, c_both, slope = [ring(slots, lambda k: f[level, k, :, at]) for f in (cx, cx_minus, cx_both, cx_slope)]
        first, second = weights(code, 1.0, 2.0, c_minus, c_both, slope)
        value = (sweep_back if back else sweep)(value, c, first, second, 0)
        return [
            [value[n * COLS : (n + 1) * COLS, chunk * LANES : (chunk + 1) * LANES] for n in range(len(slots))]
            for chunk in range(len(pieces))
        ]

    def lat_weights(substep, row, level, slots):
        code = ring(slots, lambda k: lat_code[substep, row, 1 if k == 3 else k])
        return weights(code, 3.0, 6.0, *[ring(slots, lambda k: f[level, k]) for f in (cy_minus, cy_both, cy_slope)])

    def forward(substep, slots, out_slots):
        @pl.loop(0, tracers // together)
        def _(batch):
            members = [batch * together + n for n in range(together)]
            above = {}
            for level in range(LEVELS):
                for n, tracer in enumerate(members):
                    row = tracer * LEVELS + level
                    pieces = [
                        [q[row, k, :, chunk * LANES : (chunk + 1) * LANES] for k in slots] for chunk in range(count_w)
                    ]
                    pieces = lon_sweep(substep, row, level, slots, pieces, False)
                    blocks = {k: jnp.concatenate([piece[m] for piece in pieces], axis=1) for m, k in enumerate(slots)}
                    if substep == 1:
                        blocks[3] = squeeze(blocks[1], blocks[2])
                    value = jnp.concatenate([blocks[slot] for slot in out_slots], axis=0)
                    first, second = lat_weights(substep, row, level, out_slots)
                    value = sweep(value, ring(out_slots, lambda k: cy[level, k]), first, second, 1)
                    for m, slot in enumerate(out_slots):
                        part = value[m * COLS : (m + 1) * COLS] * inv[level, slot]
                        if level > 0:
                            part = part + elim[level, slot] * above[n, slot]
                        above[n, slot] = part
                        temp[row, slot] = part
            column = {}
            for level in range(LEVELS - 1, -1, -1):
                for n, tracer in enumerate(members):
                    row = tracer * LEVELS + level
                    for slot in out_slots:
                        value = above[n, slot]
                        if level < LEVELS - 1:
                            value = temp[row, slot] + ratio[level, slot] * value
                            above[n, slot] = value
                        if slot == 0:
                            part = cw[level] * value
                            column[n] = part if level == LEVELS - 1 else column[n] + part
                        if substep == SUBSTEPS - 1:
                            final[row] = value[:, :ROWS]
                        else:
                            q[row, slot] = value
            for n, tracer in enumerate(members):
                at = substep * tracers + tracer
                force[at] = mw_w[tracer] * (column[n] - obs_w[at])

    def backward(substep, slots, out_slots):
        @pl.loop(0, tracers // together)
        def _(batch):
            members = [batch * together + n for n in range(together)]
            above = {}
            for level in range(LEVELS):
                for n, tracer in enumerate(members):
                    row = tracer * LEVELS + level
                    for slot in slots:
                        if slot == 0:
                            value = cw[level] * force[substep * tracers + tracer]
                            if substep < SUBSTEPS - 1:
                                value = value + q[row, slot]
                        else:
                            value = q[row, slot]
                        value = value * inv[level, slot]
                        if level > 0:
                            value = value + elim[level, slot] * above[n, slot]
                        above[n, slot] = value
                        temp[row, slot] = value
            below = {}
            for level in range(LEVELS - 1, -1, -1):
                for n, tracer in enumerate(members):
                    row = tracer * LEVELS + level
                    blocks = {}
                    for slot in slots:
                        value = temp[row, slot]
                        if level < LEVELS - 1:
                            value = value + ratio[level, slot] * below[n, slot]
                        below[n, slot] = value
                    first, second = lat_weights(substep, row, level, slots)
                    value = jnp.concatenate([below[n, slot] for slot in slots], axis=0)
                    value = sweep_back(value, ring(slots, lambda k: cy[level, k]), first, second, 1)
                    for m, slot in enumerate(slots):
                        blocks[slot] = value[m * COLS : (m + 1) * COLS]
                    if substep == SUBSTEPS - 1:
                        blocks[3] = jnp.zeros_like(blocks[0])
                    if substep == 1:
                        blocks[1] = jnp.where(col_w < 4, blocks[3], 0.0)
                        blocks[2] = jnp.where(col_w < 4, 0.0, blocks[3])
                    pieces = [
                        [blocks[k][:, chunk * LANES : (chunk + 1) * LANES] for k in out_slots] for chunk in range(count_w if substep else 2)
                    ]
                    pieces = lon_sweep(substep, row, level, out_slots, pieces, True)
                    for chunk in range(len(pieces)):
                        at = slice(chunk * LANES, (chunk + 1) * LANES)
                        for m, k in enumerate(out_slots):
                            if substep == 0:
                                (grad, grad_right, grad_left)[k][row, :, at] = pieces[chunk][m]
                            else:
                                q[row, k, :, at] = pieces[chunk][m]

    three, two = ((0, 1, 2), (0, 3))
    forward(0, three, three)
    forward(1, three, two)
    forward(2, two, two)
    forward(3, two, (0,))
    backward(3, (0,), two)
    backward(2, two, two)
    backward(1, two, three)
    backward(0, three, three)


def halves(half, *refs):
    own, (left_a, right_a), (north, south, corner_l, corner_r) = (refs[:8], refs[8:10], refs[10:14])
    refs = refs[14:]
    edges = (
        (north, lambda k: south[k]),
        (corner_l, lambda k: corner_l[CORNER + k]),
        (corner_r, lambda k: corner_r[CORNER + k]),
    )
    if half == 0:
        outs, scratch = (refs[:4], refs[4:])
        groups = [(0, left_a, right_a, left_a, right_a)]
    else:
        left_b, right_b, before = refs[:3]
        final, outs, scratch = (refs[3], refs[4:7], refs[7:])
        final[0:HALF] = before[...]
        outs = (final.at[HALF:STATE],) + tuple(outs)
        groups = [(PAIR, left_b, right_b, left_a, right_a)]
    window(groups, own, edges, outs, scratch)


def finish(*refs):
    out = refs[6]
    for half in range(2):
        own, right, left = refs[3 * half : 3 * half + 3]

        @pl.loop(0, HALF)
        def _(row):
            out[half * HALF + row] = own[row] + right[row] + left[row]


def spec(count, space=pltpu.VMEM):
    return [pl.BlockSpec(memory_space=space)] * count


def scratch_for(width, tracers):
    rows = tracers * LEVELS
    sizes = [(rows, 4)] * 2 + [(SUBSTEPS, rows, 3)] * 2 + [(LEVELS, 4)] * 11 + [(SUBSTEPS * tracers,), (tracers,), (SUBSTEPS * tracers,)]
    return [pltpu.VMEM(size + (COLS, width), jnp.float32) for size in sizes]


def shards(
    checkpoint, courant_lon, courant_lat, mixing, limiter_flags, column_weights, observations, misfit_weight
):
    def block(rows, lanes=ROWS):
        return jax.ShapeDtypeStruct((rows, COLS, lanes), jnp.float32)

    def call(kernel, name, outs, in_specs, operands, scratch=(), limit=LIMIT):
        return pl.pallas_call(
            kernel,
            out_shape=tuple(outs),
            in_specs=in_specs,
            out_specs=tuple(spec(len(outs))),
            scratch_shapes=list(scratch),
            compiler_params=pltpu.CompilerParams(vmem_limit_bytes=limit),
            name=name,
        )(*operands)

    lat, lon = (lax.axis_size("lat"), lax.axis_size("lon"))
    east = [(i, (i + 1) % lon) for i in range(lon)]
    west = [(j, i) for i, j in east]
    up = [(i, i + 1) for i in range(lat - 1)]
    down = [(j, i) for i, j in up]
    own = (
        checkpoint.reshape((STATE, COLS, ROWS)),
        courant_lon,
        courant_lat,
        mixing,
        limiter_flags.reshape((SUBSTEPS * STATE, COLS, ROWS)),
        observations.reshape((SUBSTEPS * TRACERS, COLS, ROWS)),
        misfit_weight,
    )
    hbm = spec(1, pltpu.HBM)
    held = [pltpu.VMEM(value.shape, value.dtype) for value in own]
    right_a, right_b, left_a, left_b, to_north, to_south = call(
        pack,
        "pack",
        [block(72), block(48), block(64), block(40), block(26, LANES), block(26, LANES)],
        hbm * 7,
        own,
        held + [pltpu.SemaphoreType.DMA((7,))],
        limit=PACK_LIMIT,
    )
    south = lax.ppermute(to_north, "lat", up)
    north = lax.ppermute(to_south, "lat", down)
    from_left_a = lax.ppermute(right_a, "lon", east)
    from_right_a = lax.ppermute(left_a, "lon", west)
    (corner,) = call(join, "join", [block(2 * CORNER, LANES)], spec(9), own + (north, south))
    corner_l = lax.ppermute(corner, "lon", east)
    corner_r = lax.ppermute(corner, "lon", west)
    corner_l, corner_r, right_b, left_b = lax.optimization_barrier((corner_l, corner_r, right_b, left_b))
    from_left_b = lax.ppermute(right_b, "lon", east)
    from_right_b = lax.ppermute(left_b, "lon", west)
    smem = spec(1, pltpu.SMEM)
    operands = own + (column_weights, from_left_a, from_right_a, north, south, corner_l, corner_r)
    final_a, grad_a, gl_a, gr_a = call(
        functools.partial(halves, 0), "window_first", [block(HALF)] * 4, spec(7) + smem + spec(6), operands,
        scratch_for(ROWS + LANES, PAIR),
    )
    from_right_1 = lax.ppermute(gl_a, "lon", west)
    from_left_1 = lax.ppermute(gr_a, "lon", east)
    final, grad_b, gl_b, gr_b = call(
        functools.partial(halves, 1), "window_second", [block(STATE)] + [block(HALF)] * 3, spec(7) + smem + spec(9),
        operands + (from_left_b, from_right_b, final_a), scratch_for(ROWS + LANES, PAIR),
    )
    from_right_2 = lax.ppermute(gl_b, "lon", west)
    from_left_2 = lax.ppermute(gr_b, "lon", east)
    (grad,) = call(
        finish, "finish", [block(STATE)], spec(6),
        (grad_a, from_right_1, from_left_1, grad_b, from_right_2, from_left_2),
    )
    return (final.reshape(checkpoint.shape), grad.reshape(checkpoint.shape))


def solution(mesh):
    return jax.shard_map(
        shards,
        mesh=mesh,
        in_specs=(
            P(None, None, "lon", "lat"),
            P(None, "lon", "lat"),
            P(None, "lon", "lat"),
            P(None, "lon", "lat"),
            P(None, None, None, "lon", "lat"),
            P(),
            P(None, None, "lon", "lat"),
            P(None, "lon", "lat"),
        ),
        out_specs=(P(None, None, "lon", "lat"), P(None, None, "lon", "lat")),
        check_vma=False,
    )
```

```python
import functools

import jax
import jax.numpy as jnp
from jax import lax
from jax.experimental import pallas as pl
from jax.experimental.pallas import tpu as pltpu
from jax.sharding import PartitionSpec as P

TRACERS, LEVELS, SUBSTEPS = 4, 8, 4
PAIR = 2
COLS, ROWS, EDGE, LANES = 8, 256, 16, 128
STATE = TRACERS * LEVELS
HALF = PAIR * LEVELS
LIMIT = 24 * 1024 * 1024
PACK_LIMIT = 60 * 1024 * 1024
CORNER = 23


def lane_ids():
    return lax.broadcasted_iota(jnp.int32, (COLS, LANES), 1)


def col_ids(lanes=LANES):
    return lax.broadcasted_iota(jnp.int32, (COLS, lanes), 0)


def fetch(hbm, own, sems):
    copies = [pltpu.make_async_copy(source, target, sems.at[k]) for k, (source, target) in enumerate(zip(hbm, own))]
    for copy in copies:
        copy.start()
    for copy in copies:
        copy.wait()


def pack(*refs):
    hbm, (right_a, right_b, left_a, left_b, to_north, to_south), own, sems = (refs[:7], refs[7:13], refs[13:20], refs[20])
    fetch(hbm, own, sems)
    ck, cl, ct, mx, fl, obs, mw = own
    lane = lane_ids()
    col = col_ids(ROWS)
    for half, (to_right, to_left) in enumerate(((right_a, left_a), (right_b, left_b))):
        to_right[0:HALF] = ck[half * HALF : (half + 1) * HALF]
        to_left[0:HALF] = ck[half * HALF : (half + 1) * HALF]

        @pl.loop(0, PAIR)
        def _(tracer):
            for level in range(LEVELS):
                row = tracer * LEVELS + level
                one, two, three, four = [
                    fl[s * STATE + half * HALF + row].astype(jnp.float32) for s in range(SUBSTEPS)
                ]
                to_right[HALF + row] = jnp.where(col >= 1, one, pltpu.roll(four, 1, 0))
                to_right[2 * HALF + row] = jnp.where(col >= 3, two, pltpu.roll(three, 3, 0))
                to_left[HALF + row] = jnp.where(col < 6, one, pltpu.roll(three, 6, 0))
                if level < 4:
                    other = fl[STATE + half * HALF + row + 4].astype(jnp.float32)
                    to_left[2 * HALF + tracer * 4 + level] = jnp.where(col < 4, two, pltpu.roll(other, 4, 0))

    for k, field in enumerate((cl, ct, mx)):
        right_a[3 * HALF + 8 * k : 3 * HALF + 8 * k + 8] = field[...]
        left_a[40 + 8 * k : 48 + 8 * k] = field[...]

    def strips(place, read, count):
        north = jnp.zeros((COLS, LANES), jnp.float32)
        south = north
        for k in range(count):
            whole = read(k)
            here = lane // EDGE
            north = jnp.where(here == (k + 7) % 8, pltpu.roll(whole[:, LANES:], EDGE * k, 1), north)
            south = jnp.where(here == k, pltpu.roll(whole[:, :LANES], EDGE * k, 1), south)
        to_north[place] = north
        to_south[place] = south

    @pl.loop(0, TRACERS)
    def _(tracer):
        strips(tracer, lambda k: ck[tracer * LEVELS + k], LEVELS)

    for place, field in ((4, cl), (5, ct), (6, mx)):
        strips(place, lambda k, field=field: field[k], LEVELS)

    @pl.loop(0, SUBSTEPS * TRACERS)
    def _(block):
        strips(7 + block, lambda k: fl[block * LEVELS + k].astype(jnp.float32), LEVELS)

    for half in range(2):
        strips(23 + half, lambda k, half=half: obs[half * 8 + k], 8)
    strips(25, lambda k: mw[k], TRACERS)


def join(*refs):
    north, south, out = (refs[7], refs[8], refs[9])
    out[0:CORNER] = north[0:CORNER]
    out[CORNER : 2 * CORNER] = south[0:CORNER]


def behind(value, axis):
    return pltpu.roll(value, 1, axis)


def ahead(value, axis):
    return pltpu.roll(value, value.shape[axis] - 1, axis)


def weights(branch, low, high, c_minus, c_both, slope):
    first = jnp.where(branch >= high, c_minus, jnp.where(branch >= low, c_both, c_minus))
    return first, jnp.where(branch >= high, slope, 0.0)


def sweep(value, courant, first, second, axis):
    step = ahead(value, axis) - value
    farther = jnp.where(courant >= 0.0, behind(step, axis), ahead(step, axis))
    flux = courant * value + first * step + second * farther
    return value - flux + behind(flux, axis)


def sweep_back(value, courant, first, second, axis):
    step = ahead(value, axis) - value
    reach = second * step
    forward = jnp.where(courant >= 0.0, reach, 0.0)
    total = first * step + ahead(forward, axis) + behind(reach - forward, axis)
    return value + courant * step + behind(total, axis) - total


def slopes(courant):
    c_minus = jnp.minimum(courant, 0.0)
    size = jnp.abs(courant)
    slope = 0.5 * size * (1.0 - size)
    return c_minus, c_minus + slope, slope


def window(groups, own, edges, outs, scratch):
    width, together = (ROWS + LANES, 1)
    ck, cl, ct, mx, fl, obs, mw, cw = own
    final, grad, grad_left, grad_right = outs
    (
        q, temp, lon_code, lat_code, cx, cx_minus, cx_both, cx_slope, cy, cy_minus, cy_both, cy_slope,
        inv, elim, ratio, obs_w, mw_w, force,
    ) = scratch
    lane, col_w = (lane_ids(), col_ids(width))
    strip_of = lane // EDGE
    rim = (lane < EDGE) | (lane >= LANES - EDGE)
    count_w = width // LANES
    tracers = PAIR * len(groups)
    offset = groups[0][0]
    static_left, static_right = groups[0][3:5]

    def spread(value, which, place, k):
        north, south = edges[which]
        halo = pltpu.roll(jnp.where(strip_of == k, north[place], south(place)), (LANES - EDGE * k) % LANES, 1)
        return jnp.concatenate([value, jnp.where(rim, halo, 0.0)], axis=1)

    def squeeze(right, left):
        return jnp.where(col_w < 4, right, left)

    lane_w = lax.broadcasted_iota(jnp.int32, (COLS, width), 1)
    last = lax.axis_index("lat") == lax.axis_size("lat") - 1
    pole = (lane_w == ROWS - 1) & last
    carry = [None] * 4
    for level in range(LEVELS):
        def blocks(field, k):
            own_block = spread(field[level], 0, 4 + k, level)
            right = spread(static_right[40 + 8 * k + level], 2, 4 + k, level)
            left = spread(static_left[48 + 8 * k + level], 1, 4 + k, level)
            return [own_block, right, left, squeeze(right, left)]

        for k, value in enumerate(blocks(cl, 0)):
            cx[level, k] = value
            cx_minus[level, k], cx_both[level, k], cx_slope[level, k] = slopes(value)
        for k, value in enumerate(blocks(ct, 1)):
            value = jnp.where(pole, 0.0, value)
            cy[level, k] = value
            cy_minus[level, k], cy_both[level, k], cy_slope[level, k] = slopes(value)
        for k, value in enumerate(blocks(mx, 2)):
            coupling = value if level < LEVELS - 1 else jnp.zeros_like(value)
            pivot = 1.0 + coupling
            if level > 0:
                above, above_ratio = carry[k]
                pivot = pivot + above - above * above_ratio
            inverse = 1.0 / pivot
            inv[level, k] = inverse
            ratio[level, k] = coupling * inverse
            elim[level, k] = above * inverse if level > 0 else jnp.zeros_like(value)
            carry[k] = (coupling, coupling * inverse)

    for substep in range(SUBSTEPS):
        for tracer in range(tracers):
            k = substep * TRACERS + offset + tracer
            obs_w[substep * tracers + tracer] = spread(obs[k], 0, 23 + k // 8, k % 8)
    for tracer in range(tracers):
        mw_w[tracer] = spread(mw[offset + tracer], 0, 25, offset + tracer)

    def put_codes(substep, row, blocks, lat_blocks):
        for k, value in enumerate(blocks):
            lon_code[substep, row, k] = value - jnp.where(value >= 6.0, 6.0, jnp.where(value >= 3.0, 3.0, 0.0))
        for k, value in enumerate(lat_blocks):
            lat_code[substep, row, k] = value

    for first, from_left, from_right, _, _ in groups:
        @pl.loop(0, PAIR)
        def _(within):
            for level in range(LEVELS):
                part = within * LEVELS + level
                row = (first - offset) * LEVELS + part
                whole = first * LEVELS + part
                place = first + within
                q[row, 0] = spread(ck[whole], 0, place, level)
                q[row, 1] = spread(from_right[part], 2, place, level)
                q[row, 2] = spread(from_left[part], 1, place, level)

                def tail(value, which, s):
                    return spread(value, which, 7 + s * TRACERS + place, level)

                mine = [tail(fl[s * STATE + whole].astype(jnp.float32), 0, s) for s in range(SUBSTEPS)]
                l_a, l_b = (from_left[HALF + part], from_left[2 * HALF + part])
                r_a = from_right[HALF + part]
                r_b = from_right[2 * HALF + within * 4 + level % 4]
                if level >= 4:
                    r_b = pltpu.roll(r_b, 4, 0)
                one = [mine[0], tail(r_a, 2, 0), tail(l_a, 1, 0)]
                put_codes(0, row, one, one)
                two = [mine[1], tail(r_b, 2, 1), tail(l_b, 1, 1)]
                put_codes(1, row, two, [mine[1], squeeze(two[1], two[2])])
                three = [
                    mine[2], squeeze(tail(pltpu.roll(r_a, 2, 0), 2, 2), tail(pltpu.roll(l_b, 5, 0), 1, 2))
                ]
                put_codes(2, row, three, three)
                four = [mine[3], tail(pltpu.roll(l_a, 7, 0), 1, 3)]
                put_codes(3, row, four, [mine[3]])

    def ring(slots, read):
        return jnp.concatenate([read(k) for k in slots], axis=0)

    def lon_sweep(substep, row, level, slots, pieces, back):
        code_slots = slots if len(slots) == 3 else (0, 1)
        at = slice(0, len(pieces) * LANES)
        value = jnp.concatenate([jnp.concatenate(piece, axis=0) for piece in pieces], axis=1)
        code = ring(code_slots, lambda k: lon_code[substep, row, k, :, at])
        c, c_minus, c_both, slope = [ring(slots, lambda k: f[level, k, :, at]) for f in (cx, cx_minus, cx_both, cx_slope)]
        first, second = weights(code, 1.0, 2.0, c_minus, c_both, slope)
        value = (sweep_back if back else sweep)(value, c, first, second, 0)
        return [
            [value[n * COLS : (n + 1) * COLS, chunk * LANES : (chunk + 1) * LANES] for n in range(len(slots))]
            for chunk in range(len(pieces))
        ]

    def lat_weights(substep, row, level, slots):
        code = ring(slots, lambda k: lat_code[substep, row, 1 if k == 3 else k])
        return weights(code, 3.0, 6.0, *[ring(slots, lambda k: f[level, k]) for f in (cy_minus, cy_both, cy_slope)])

    def forward(substep, slots, out_slots):
        @pl.loop(0, tracers // together)
        def _(batch):
            members = [batch * together + n for n in range(together)]
            above = {}
            for level in range(LEVELS):
                for n, tracer in enumerate(members):
                    row = tracer * LEVELS + level
                    pieces = [
                        [q[row, k, :, chunk * LANES : (chunk + 1) * LANES] for k in slots] for chunk in range(count_w)
                    ]
                    pieces = lon_sweep(substep, row, level, slots, pieces, False)
                    blocks = {k: jnp.concatenate([piece[m] for piece in pieces], axis=1) for m, k in enumerate(slots)}
                    if substep == 1:
                        blocks[3] = squeeze(blocks[1], blocks[2])
                    value = jnp.concatenate([blocks[slot] for slot in out_slots], axis=0)
                    first, second = lat_weights(substep, row, level, out_slots)
                    value = sweep(value, ring(out_slots, lambda k: cy[level, k]), first, second, 1)
                    for m, slot in enumerate(out_slots):
                        part = value[m * COLS : (m + 1) * COLS] * inv[level, slot]
                        if level > 0:
                            part = part + elim[level, slot] * above[n, slot]
                        above[n, slot] = part
                        temp[row, slot] = part
            column = {}
            for level in range(LEVELS - 1, -1, -1):
                for n, tracer in enumerate(members):
                    row = tracer * LEVELS + level
                    for slot in out_slots:
                        value = above[n, slot]
                        if level < LEVELS - 1:
                            value = temp[row, slot] + ratio[level, slot] * value
                            above[n, slot] = value
                        if slot == 0:
                            part = cw[level] * value
                            column[n] = part if level == LEVELS - 1 else column[n] + part
                        if substep == SUBSTEPS - 1:
                            final[row] = value[:, :ROWS]
                        else:
                            q[row, slot] = value
            for n, tracer in enumerate(members):
                at = substep * tracers + tracer
                force[at] = mw_w[tracer] * (column[n] - obs_w[at])

    def backward(substep, slots, out_slots):
        @pl.loop(0, tracers // together)
        def _(batch):
            members = [batch * together + n for n in range(together)]
            above = {}
            for level in range(LEVELS):
                for n, tracer in enumerate(members):
                    row = tracer * LEVELS + level
                    for slot in slots:
                        if slot == 0:
                            value = cw[level] * force[substep * tracers + tracer]
                            if substep < SUBSTEPS - 1:
                                value = value + q[row, slot]
                        else:
                            value = q[row, slot]
                        value = value * inv[level, slot]
                        if level > 0:
                            value = value + elim[level, slot] * above[n, slot]
                        above[n, slot] = value
                        temp[row, slot] = value
            below = {}
            for level in range(LEVELS - 1, -1, -1):
                for n, tracer in enumerate(members):
                    row = tracer * LEVELS + level
                    blocks = {}
                    for slot in slots:
                        value = temp[row, slot]
                        if level < LEVELS - 1:
                            value = value + ratio[level, slot] * below[n, slot]
                        below[n, slot] = value
                    first, second = lat_weights(substep, row, level, slots)
                    value = jnp.concatenate([below[n, slot] for slot in slots], axis=0)
                    value = sweep_back(value, ring(slots, lambda k: cy[level, k]), first, second, 1)
                    for m, slot in enumerate(slots):
                        blocks[slot] = value[m * COLS : (m + 1) * COLS]
                    if substep == SUBSTEPS - 1:
                        blocks[3] = jnp.zeros_like(blocks[0])
                    if substep == 1:
                        blocks[1] = jnp.where(col_w < 4, blocks[3], 0.0)
                        blocks[2] = jnp.where(col_w < 4, 0.0, blocks[3])
                    pieces = [
                        [blocks[k][:, chunk * LANES : (chunk + 1) * LANES] for k in out_slots] for chunk in range(count_w if substep else 2)
                    ]
                    pieces = lon_sweep(substep, row, level, out_slots, pieces, True)
                    for chunk in range(len(pieces)):
                        at = slice(chunk * LANES, (chunk + 1) * LANES)
                        for m, k in enumerate(out_slots):
                            if substep == 0:
                                (grad, grad_right, grad_left)[k][row, :, at] = pieces[chunk][m]
                            else:
                                q[row, k, :, at] = pieces[chunk][m]

    three, two = ((0, 1, 2), (0, 3))
    forward(0, three, three)
    forward(1, three, two)
    forward(2, two, two)
    forward(3, two, (0,))
    backward(3, (0,), two)
    backward(2, two, two)
    backward(1, two, three)
    backward(0, three, three)


def halves(half, *refs):
    own, (left_a, right_a), (north, south, corner_l, corner_r) = (refs[:8], refs[8:10], refs[10:14])
    refs = refs[14:]
    edges = (
        (north, lambda k: south[k]),
        (corner_l, lambda k: corner_l[CORNER + k]),
        (corner_r, lambda k: corner_r[CORNER + k]),
    )
    if half == 0:
        outs, scratch = (refs[:4], refs[4:])
        groups = [(0, left_a, right_a, left_a, right_a)]
    else:
        left_b, right_b, before = refs[:3]
        final, outs, scratch = (refs[3], refs[4:7], refs[7:])
        final[0:HALF] = before[...]
        outs = (final.at[HALF:STATE],) + tuple(outs)
        groups = [(PAIR, left_b, right_b, left_a, right_a)]
    window(groups, own, edges, outs, scratch)


def finish(*refs):
    out = refs[6]
    for half in range(2):
        own, right, left = refs[3 * half : 3 * half + 3]

        @pl.loop(0, HALF)
        def _(row):
            out[half * HALF + row] = own[row] + right[row] + left[row]


def spec(count, space=pltpu.VMEM):
    return [pl.BlockSpec(memory_space=space)] * count


def scratch_for(width, tracers):
    rows = tracers * LEVELS
    sizes = [(rows, 4)] * 2 + [(SUBSTEPS, rows, 3)] * 2 + [(LEVELS, 4)] * 11 + [(SUBSTEPS * tracers,), (tracers,), (SUBSTEPS * tracers,)]
    return [pltpu.VMEM(size + (COLS, width), jnp.float32) for size in sizes]


def shards(
    checkpoint, courant_lon, courant_lat, mixing, limiter_flags, column_weights, observations, misfit_weight
):
    def block(rows, lanes=ROWS):
        return jax.ShapeDtypeStruct((rows, COLS, lanes), jnp.float32)

    def call(kernel, name, outs, in_specs, operands, scratch=(), limit=LIMIT):
        return pl.pallas_call(
            kernel,
            out_shape=tuple(outs),
            in_specs=in_specs,
            out_specs=tuple(spec(len(outs))),
            scratch_shapes=list(scratch),
            compiler_params=pltpu.CompilerParams(vmem_limit_bytes=limit),
            name=name,
        )(*operands)

    lat, lon = (lax.axis_size("lat"), lax.axis_size("lon"))
    east = [(i, (i + 1) % lon) for i in range(lon)]
    west = [(j, i) for i, j in east]
    up = [(i, i + 1) for i in range(lat - 1)]
    down = [(j, i) for i, j in up]
    own = (
        checkpoint.reshape((STATE, COLS, ROWS)),
        courant_lon,
        courant_lat,
        mixing,
        limiter_flags.reshape((SUBSTEPS * STATE, COLS, ROWS)),
        observations.reshape((SUBSTEPS * TRACERS, COLS, ROWS)),
        misfit_weight,
    )
    hbm = spec(1, pltpu.HBM)
    held = [pltpu.VMEM(value.shape, value.dtype) for value in own]
    right_a, right_b, left_a, left_b, to_north, to_south = call(
        pack,
        "pack",
        [block(72), block(48), block(64), block(40), block(26, LANES), block(26, LANES)],
        hbm * 7,
        own,
        held + [pltpu.SemaphoreType.DMA((7,))],
        limit=PACK_LIMIT,
    )
    south = lax.ppermute(to_north, "lat", up)
    north = lax.ppermute(to_south, "lat", down)
    from_left_a = lax.ppermute(right_a, "lon", east)
    from_right_a = lax.ppermute(left_a, "lon", west)
    (corner,) = call(join, "join", [block(2 * CORNER, LANES)], spec(9), own + (north, south))
    corner_l = lax.ppermute(corner, "lon", east)
    corner_r = lax.ppermute(corner, "lon", west)
    from_right_a, corner_l, corner_r, right_b, left_b = lax.optimization_barrier(
        (from_right_a, corner_l, corner_r, right_b, left_b)
    )
    from_left_b = lax.ppermute(right_b, "lon", east)
    from_right_b = lax.ppermute(left_b, "lon", west)
    smem = spec(1, pltpu.SMEM)
    operands = own + (column_weights, from_left_a, from_right_a, north, south, corner_l, corner_r)
    final_a, grad_a, gl_a, gr_a = call(
        functools.partial(halves, 0), "window_first", [block(HALF)] * 4, spec(7) + smem + spec(6), operands,
        scratch_for(ROWS + LANES, PAIR),
    )
    from_right_1 = lax.ppermute(gl_a, "lon", west)
    from_left_1 = lax.ppermute(gr_a, "lon", east)
    final, grad_b, gl_b, gr_b = call(
        functools.partial(halves, 1), "window_second", [block(STATE)] + [block(HALF)] * 3, spec(7) + smem + spec(9),
        operands + (from_left_b, from_right_b, final_a), scratch_for(ROWS + LANES, PAIR),
    )
    from_right_2 = lax.ppermute(gl_b, "lon", west)
    from_left_2 = lax.ppermute(gr_b, "lon", east)
    (grad,) = call(
        finish, "finish", [block(STATE)], spec(6),
        (grad_a, from_right_1, from_left_1, grad_b, from_right_2, from_left_2),
    )
    return (final.reshape(checkpoint.shape), grad.reshape(checkpoint.shape))


def solution(mesh):
    return jax.shard_map(
        shards,
        mesh=mesh,
        in_specs=(
            P(None, None, "lon", "lat"),
            P(None, "lon", "lat"),
            P(None, "lon", "lat"),
            P(None, "lon", "lat"),
            P(None, None, None, "lon", "lat"),
            P(),
            P(None, None, "lon", "lat"),
            P(None, "lon", "lat"),
        ),
        out_specs=(P(None, None, "lon", "lat"), P(None, None, "lon", "lat")),
        check_vma=False,
    )
```

```python
import functools

import jax
import jax.numpy as jnp
from jax import lax
from jax.experimental import pallas as pl
from jax.experimental.pallas import tpu as pltpu
from jax.sharding import PartitionSpec as P

TRACERS, LEVELS, SUBSTEPS = 4, 8, 4
PAIR = 2
BATCH = 2
COLS, ROWS, EDGE, LANES = 8, 256, 16, 128
STATE = TRACERS * LEVELS
HALF = PAIR * LEVELS
LIMIT = 24 * 1024 * 1024
PACK_LIMIT = 60 * 1024 * 1024
CORNER = 23


def lane_ids():
    return lax.broadcasted_iota(jnp.int32, (COLS, LANES), 1)


def col_ids(lanes=LANES):
    return lax.broadcasted_iota(jnp.int32, (COLS, lanes), 0)


def fetch(hbm, own, sems):
    copies = [pltpu.make_async_copy(source, target, sems.at[k]) for k, (source, target) in enumerate(zip(hbm, own))]
    for copy in copies:
        copy.start()
    for copy in copies:
        copy.wait()


def pack(*refs):
    hbm, (right_a, right_b, left_a, left_b, to_north, to_south), own, sems = (refs[:7], refs[7:13], refs[13:20], refs[20])
    fetch(hbm, own, sems)
    ck, cl, ct, mx, fl, obs, mw = own
    lane = lane_ids()
    col = col_ids(ROWS)
    for half, (to_right, to_left) in enumerate(((right_a, left_a), (right_b, left_b))):
        to_right[0:HALF] = ck[half * HALF : (half + 1) * HALF]
        to_left[0:HALF] = ck[half * HALF : (half + 1) * HALF]

        @pl.loop(0, PAIR)
        def _(tracer):
            for level in range(LEVELS):
                row = tracer * LEVELS + level
                one, two, three, four = [
                    fl[s * STATE + half * HALF + row].astype(jnp.float32) for s in range(SUBSTEPS)
                ]
                to_right[HALF + row] = jnp.where(col >= 1, one, pltpu.roll(four, 1, 0))
                to_right[2 * HALF + row] = jnp.where(col >= 3, two, pltpu.roll(three, 3, 0))
                to_left[HALF + row] = jnp.where(col < 6, one, pltpu.roll(three, 6, 0))
                if level < 4:
                    other = fl[STATE + half * HALF + row + 4].astype(jnp.float32)
                    to_left[2 * HALF + tracer * 4 + level] = jnp.where(col < 4, two, pltpu.roll(other, 4, 0))

    for k, field in enumerate((cl, ct, mx)):
        right_a[3 * HALF + 8 * k : 3 * HALF + 8 * k + 8] = field[...]
        left_a[40 + 8 * k : 48 + 8 * k] = field[...]

    def strips(place, read, count):
        north = jnp.zeros((COLS, LANES), jnp.float32)
        south = north
        for k in range(count):
            whole = read(k)
            here = lane // EDGE
            north = jnp.where(here == (k + 7) % 8, pltpu.roll(whole[:, LANES:], EDGE * k, 1), north)
            south = jnp.where(here == k, pltpu.roll(whole[:, :LANES], EDGE * k, 1), south)
        to_north[place] = north
        to_south[place] = south

    @pl.loop(0, TRACERS)
    def _(tracer):
        strips(tracer, lambda k: ck[tracer * LEVELS + k], LEVELS)

    for place, field in ((4, cl), (5, ct), (6, mx)):
        strips(place, lambda k, field=field: field[k], LEVELS)

    @pl.loop(0, SUBSTEPS * TRACERS)
    def _(block):
        strips(7 + block, lambda k: fl[block * LEVELS + k].astype(jnp.float32), LEVELS)

    for half in range(2):
        strips(23 + half, lambda k, half=half: obs[half * 8 + k], 8)
    strips(25, lambda k: mw[k], TRACERS)


def join(*refs):
    north, south, out = (refs[7], refs[8], refs[9])
    out[0:CORNER] = north[0:CORNER]
    out[CORNER : 2 * CORNER] = south[0:CORNER]


def behind(value, axis):
    return pltpu.roll(value, 1, axis)


def ahead(value, axis):
    return pltpu.roll(value, value.shape[axis] - 1, axis)


def weights(branch, low, high, c_minus, c_both, slope):
    first = jnp.where(branch >= high, c_minus, jnp.where(branch >= low, c_both, c_minus))
    return first, jnp.where(branch >= high, slope, 0.0)


def sweep(value, courant, first, second, axis):
    step = ahead(value, axis) - value
    farther = jnp.where(courant >= 0.0, behind(step, axis), ahead(step, axis))
    flux = courant * value + first * step + second * farther
    return value - flux + behind(flux, axis)


def sweep_back(value, courant, first, second, axis):
    step = ahead(value, axis) - value
    reach = second * step
    forward = jnp.where(courant >= 0.0, reach, 0.0)
    total = first * step + ahead(forward, axis) + behind(reach - forward, axis)
    return value + courant * step + behind(total, axis) - total


def slopes(courant):
    c_minus = jnp.minimum(courant, 0.0)
    size = jnp.abs(courant)
    slope = 0.5 * size * (1.0 - size)
    return c_minus, c_minus + slope, slope


def window(groups, own, edges, outs, scratch):
    width, together = (ROWS + LANES, 1)
    ck, cl, ct, mx, fl, obs, mw, cw = own
    final, grad, grad_left, grad_right = outs
    (
        q, temp, lon_code, lat_code, cx, cx_minus, cx_both, cx_slope, cy, cy_minus, cy_both, cy_slope,
        inv, elim, ratio, obs_w, mw_w, force,
    ) = scratch
    lane, col_w = (lane_ids(), col_ids(width))
    strip_of = lane // EDGE
    rim = (lane < EDGE) | (lane >= LANES - EDGE)
    count_w = width // LANES
    tracers = PAIR * len(groups)
    offset = groups[0][0]
    static_left, static_right = groups[0][3:5]

    def spread(value, which, place, k):
        north, south = edges[which]
        halo = pltpu.roll(jnp.where(strip_of == k, north[place], south(place)), (LANES - EDGE * k) % LANES, 1)
        return jnp.concatenate([value, jnp.where(rim, halo, 0.0)], axis=1)

    def squeeze(right, left):
        return jnp.where(col_w < 4, right, left)

    lane_w = lax.broadcasted_iota(jnp.int32, (COLS, width), 1)
    last = lax.axis_index("lat") == lax.axis_size("lat") - 1
    pole = (lane_w == ROWS - 1) & last
    carry = [None] * 4
    for level in range(LEVELS):
        def blocks(field, k):
            own_block = spread(field[level], 0, 4 + k, level)
            right = spread(static_right[40 + 8 * k + level], 2, 4 + k, level)
            left = spread(static_left[48 + 8 * k + level], 1, 4 + k, level)
            return [own_block, right, left, squeeze(right, left)]

        for k, value in enumerate(blocks(cl, 0)):
            cx[level, k] = value
            cx_minus[level, k], cx_both[level, k], cx_slope[level, k] = slopes(value)
        for k, value in enumerate(blocks(ct, 1)):
            value = jnp.where(pole, 0.0, value)
            cy[level, k] = value
            cy_minus[level, k], cy_both[level, k], cy_slope[level, k] = slopes(value)
        for k, value in enumerate(blocks(mx, 2)):
            coupling = value if level < LEVELS - 1 else jnp.zeros_like(value)
            pivot = 1.0 + coupling
            if level > 0:
                above, above_ratio = carry[k]
                pivot = pivot + above - above * above_ratio
            inverse = 1.0 / pivot
            inv[level, k] = inverse
            ratio[level, k] = coupling * inverse
            elim[level, k] = above * inverse if level > 0 else jnp.zeros_like(value)
            carry[k] = (coupling, coupling * inverse)

    for substep in range(SUBSTEPS):
        for tracer in range(tracers):
            k = substep * TRACERS + offset + tracer
            obs_w[substep * tracers + tracer] = spread(obs[k], 0, 23 + k // 8, k % 8)
    for tracer in range(tracers):
        mw_w[tracer] = spread(mw[offset + tracer], 0, 25, offset + tracer)

    def put_codes(substep, row, blocks, lat_blocks):
        for k, value in enumerate(blocks):
            lon_code[substep, row, k] = value - jnp.where(value >= 6.0, 6.0, jnp.where(value >= 3.0, 3.0, 0.0))
        for k, value in enumerate(lat_blocks):
            lat_code[substep, row, k] = value

    for first, from_left, from_right, _, _ in groups:
        @pl.loop(0, PAIR)
        def _(within):
            for level in range(LEVELS):
                part = within * LEVELS + level
                row = (first - offset) * LEVELS + part
                whole = first * LEVELS + part
                place = first + within
                q[row, 0] = spread(ck[whole], 0, place, level)
                q[row, 1] = spread(from_right[part], 2, place, level)
                q[row, 2] = spread(from_left[part], 1, place, level)

                def tail(value, which, s):
                    return spread(value, which, 7 + s * TRACERS + place, level)

                mine = [tail(fl[s * STATE + whole].astype(jnp.float32), 0, s) for s in range(SUBSTEPS)]
                l_a, l_b = (from_left[HALF + part], from_left[2 * HALF + part])
                r_a = from_right[HALF + part]
                r_b = from_right[2 * HALF + within * 4 + level % 4]
                if level >= 4:
                    r_b = pltpu.roll(r_b, 4, 0)
                one = [mine[0], tail(r_a, 2, 0), tail(l_a, 1, 0)]
                put_codes(0, row, one, one)
                two = [mine[1], tail(r_b, 2, 1), tail(l_b, 1, 1)]
                put_codes(1, row, two, [mine[1], squeeze(two[1], two[2])])
                three = [
                    mine[2], squeeze(tail(pltpu.roll(r_a, 2, 0), 2, 2), tail(pltpu.roll(l_b, 5, 0), 1, 2))
                ]
                put_codes(2, row, three, three)
                four = [mine[3], tail(pltpu.roll(l_a, 7, 0), 1, 3)]
                put_codes(3, row, four, [mine[3]])

    def ring(slots, read):
        return jnp.concatenate([read(k) for k in slots], axis=0)

    def lon_sweep(substep, row, level, slots, pieces, back):
        code_slots = slots if len(slots) == 3 else (0, 1)
        at = slice(0, len(pieces) * LANES)
        value = jnp.concatenate([jnp.concatenate(piece, axis=0) for piece in pieces], axis=1)
        code = ring(code_slots, lambda k: lon_code[substep, row, k, :, at])
        c, c_minus, c_both, slope = [ring(slots, lambda k: f[level, k, :, at]) for f in (cx, cx_minus, cx_both, cx_slope)]
        first, second = weights(code, 1.0, 2.0, c_minus, c_both, slope)
        value = (sweep_back if back else sweep)(value, c, first, second, 0)
        return [
            [value[n * COLS : (n + 1) * COLS, chunk * LANES : (chunk + 1) * LANES] for n in range(len(slots))]
            for chunk in range(len(pieces))
        ]

    def lat_weights(substep, row, level, slots):
        code = ring(slots, lambda k: lat_code[substep, row, 1 if k == 3 else k])
        return weights(code, 3.0, 6.0, *[ring(slots, lambda k: f[level, k]) for f in (cy_minus, cy_both, cy_slope)])

    def forward(substep, slots, out_slots):
        @pl.loop(0, tracers // together)
        def _(batch):
            members = [batch * together + n for n in range(together)]
            above = {}
            stacked = []
            for level in range(LEVELS):
                for n, tracer in enumerate(members):
                    row = tracer * LEVELS + level
                    pieces = [
                        [q[row, k, :, chunk * LANES : (chunk + 1) * LANES] for k in slots] for chunk in range(count_w)
                    ]
                    pieces = lon_sweep(substep, row, level, slots, pieces, False)
                    blocks = {k: jnp.concatenate([piece[m] for piece in pieces], axis=1) for m, k in enumerate(slots)}
                    if substep == 1:
                        blocks[3] = squeeze(blocks[1], blocks[2])
                    stacked.append((n, row, level, blocks))
                    if len(stacked) < BATCH:
                        continue
                    value = jnp.concatenate([b[slot] for _, _, _, b in stacked for slot in out_slots], axis=0)
                    both = [lat_weights(substep, r, z, out_slots) for _, r, z, _ in stacked]
                    first, second = [jnp.concatenate([w[e] for w in both], axis=0) for e in range(2)]
                    c = jnp.concatenate([ring(out_slots, lambda k: cy[z, k]) for _, _, z, _ in stacked], axis=0)
                    value = sweep(value, c, first, second, 1)
                    m = 0
                    for n_, r, z, _ in stacked:
                        for slot in out_slots:
                            part = value[m * COLS : (m + 1) * COLS] * inv[z, slot]
                            m += 1
                            if z > 0:
                                part = part + elim[z, slot] * above[n_, slot]
                            above[n_, slot] = part
                            temp[r, slot] = part
                    stacked = []
            column = {}
            for level in range(LEVELS - 1, -1, -1):
                for n, tracer in enumerate(members):
                    row = tracer * LEVELS + level
                    for slot in out_slots:
                        value = above[n, slot]
                        if level < LEVELS - 1:
                            value = temp[row, slot] + ratio[level, slot] * value
                            above[n, slot] = value
                        if slot == 0:
                            part = cw[level] * value
                            column[n] = part if level == LEVELS - 1 else column[n] + part
                        if substep == SUBSTEPS - 1:
                            final[row] = value[:, :ROWS]
                        else:
                            q[row, slot] = value
            for n, tracer in enumerate(members):
                at = substep * tracers + tracer
                force[at] = mw_w[tracer] * (column[n] - obs_w[at])

    def backward(substep, slots, out_slots):
        @pl.loop(0, tracers // together)
        def _(batch):
            members = [batch * together + n for n in range(together)]
            above = {}
            for level in range(LEVELS):
                for n, tracer in enumerate(members):
                    row = tracer * LEVELS + level
                    for slot in slots:
                        if slot == 0:
                            value = cw[level] * force[substep * tracers + tracer]
                            if substep < SUBSTEPS - 1:
                                value = value + q[row, slot]
                        else:
                            value = q[row, slot]
                        value = value * inv[level, slot]
                        if level > 0:
                            value = value + elim[level, slot] * above[n, slot]
                        above[n, slot] = value
                        temp[row, slot] = value
            below = {}
            for level in range(LEVELS - 1, -1, -1):
                for n, tracer in enumerate(members):
                    row = tracer * LEVELS + level
                    blocks = {}
                    for slot in slots:
                        value = temp[row, slot]
                        if level < LEVELS - 1:
                            value = value + ratio[level, slot] * below[n, slot]
                        below[n, slot] = value
                    first, second = lat_weights(substep, row, level, slots)
                    value = jnp.concatenate([below[n, slot] for slot in slots], axis=0)
                    value = sweep_back(value, ring(slots, lambda k: cy[level, k]), first, second, 1)
                    for m, slot in enumerate(slots):
                        blocks[slot] = value[m * COLS : (m + 1) * COLS]
                    if substep == SUBSTEPS - 1:
                        blocks[3] = jnp.zeros_like(blocks[0])
                    if substep == 1:
                        blocks[1] = jnp.where(col_w < 4, blocks[3], 0.0)
                        blocks[2] = jnp.where(col_w < 4, 0.0, blocks[3])
                    pieces = [
                        [blocks[k][:, chunk * LANES : (chunk + 1) * LANES] for k in out_slots] for chunk in range(count_w if substep else 2)
                    ]
                    pieces = lon_sweep(substep, row, level, out_slots, pieces, True)
                    for chunk in range(len(pieces)):
                        at = slice(chunk * LANES, (chunk + 1) * LANES)
                        for m, k in enumerate(out_slots):
                            if substep == 0:
                                (grad, grad_right, grad_left)[k][row, :, at] = pieces[chunk][m]
                            else:
                                q[row, k, :, at] = pieces[chunk][m]

    three, two = ((0, 1, 2), (0, 3))
    forward(0, three, three)
    forward(1, three, two)
    forward(2, two, two)
    forward(3, two, (0,))
    backward(3, (0,), two)
    backward(2, two, two)
    backward(1, two, three)
    backward(0, three, three)


def halves(half, *refs):
    own, (left_a, right_a), (north, south, corner_l, corner_r) = (refs[:8], refs[8:10], refs[10:14])
    refs = refs[14:]
    edges = (
        (north, lambda k: south[k]),
        (corner_l, lambda k: corner_l[CORNER + k]),
        (corner_r, lambda k: corner_r[CORNER + k]),
    )
    if half == 0:
        outs, scratch = (refs[:4], refs[4:])
        groups = [(0, left_a, right_a, left_a, right_a)]
    else:
        left_b, right_b, before = refs[:3]
        final, outs, scratch = (refs[3], refs[4:7], refs[7:])
        final[0:HALF] = before[...]
        outs = (final.at[HALF:STATE],) + tuple(outs)
        groups = [(PAIR, left_b, right_b, left_a, right_a)]
    window(groups, own, edges, outs, scratch)


def finish(*refs):
    out = refs[6]
    for half in range(2):
        own, right, left = refs[3 * half : 3 * half + 3]

        @pl.loop(0, HALF)
        def _(row):
            out[half * HALF + row] = own[row] + right[row] + left[row]


def spec(count, space=pltpu.VMEM):
    return [pl.BlockSpec(memory_space=space)] * count


def scratch_for(width, tracers):
    rows = tracers * LEVELS
    sizes = [(rows, 4)] * 2 + [(SUBSTEPS, rows, 3)] * 2 + [(LEVELS, 4)] * 11 + [(SUBSTEPS * tracers,), (tracers,), (SUBSTEPS * tracers,)]
    return [pltpu.VMEM(size + (COLS, width), jnp.float32) for size in sizes]


def shards(
    checkpoint, courant_lon, courant_lat, mixing, limiter_flags, column_weights, observations, misfit_weight
):
    def block(rows, lanes=ROWS):
        return jax.ShapeDtypeStruct((rows, COLS, lanes), jnp.float32)

    def call(kernel, name, outs, in_specs, operands, scratch=(), limit=LIMIT):
        return pl.pallas_call(
            kernel,
            out_shape=tuple(outs),
            in_specs=in_specs,
            out_specs=tuple(spec(len(outs))),
            scratch_shapes=list(scratch),
            compiler_params=pltpu.CompilerParams(vmem_limit_bytes=limit),
            name=name,
        )(*operands)

    lat, lon = (lax.axis_size("lat"), lax.axis_size("lon"))
    east = [(i, (i + 1) % lon) for i in range(lon)]
    west = [(j, i) for i, j in east]
    up = [(i, i + 1) for i in range(lat - 1)]
    down = [(j, i) for i, j in up]
    own = (
        checkpoint.reshape((STATE, COLS, ROWS)),
        courant_lon,
        courant_lat,
        mixing,
        limiter_flags.reshape((SUBSTEPS * STATE, COLS, ROWS)),
        observations.reshape((SUBSTEPS * TRACERS, COLS, ROWS)),
        misfit_weight,
    )
    hbm = spec(1, pltpu.HBM)
    held = [pltpu.VMEM(value.shape, value.dtype) for value in own]
    right_a, right_b, left_a, left_b, to_north, to_south = call(
        pack,
        "pack",
        [block(72), block(48), block(64), block(40), block(26, LANES), block(26, LANES)],
        hbm * 7,
        own,
        held + [pltpu.SemaphoreType.DMA((7,))],
        limit=PACK_LIMIT,
    )
    south = lax.ppermute(to_north, "lat", up)
    north = lax.ppermute(to_south, "lat", down)
    from_left_a = lax.ppermute(right_a, "lon", east)
    from_right_a = lax.ppermute(left_a, "lon", west)
    (corner,) = call(join, "join", [block(2 * CORNER, LANES)], spec(9), own + (north, south))
    corner_l = lax.ppermute(corner, "lon", east)
    corner_r = lax.ppermute(corner, "lon", west)
    from_right_a, corner_l, corner_r, right_b, left_b = lax.optimization_barrier(
        (from_right_a, corner_l, corner_r, right_b, left_b)
    )
    from_left_b = lax.ppermute(right_b, "lon", east)
    from_right_b = lax.ppermute(left_b, "lon", west)
    smem = spec(1, pltpu.SMEM)
    operands = own + (column_weights, from_left_a, from_right_a, north, south, corner_l, corner_r)
    final_a, grad_a, gl_a, gr_a = call(
        functools.partial(halves, 0), "window_first", [block(HALF)] * 4, spec(7) + smem + spec(6), operands,
        scratch_for(ROWS + LANES, PAIR),
    )
    from_right_1 = lax.ppermute(gl_a, "lon", west)
    from_left_1 = lax.ppermute(gr_a, "lon", east)
    final, grad_b, gl_b, gr_b = call(
        functools.partial(halves, 1), "window_second", [block(STATE)] + [block(HALF)] * 3, spec(7) + smem + spec(9),
        operands + (from_left_b, from_right_b, final_a), scratch_for(ROWS + LANES, PAIR),
    )
    from_right_2 = lax.ppermute(gl_b, "lon", west)
    from_left_2 = lax.ppermute(gr_b, "lon", east)
    (grad,) = call(
        finish, "finish", [block(STATE)], spec(6),
        (grad_a, from_right_1, from_left_1, grad_b, from_right_2, from_left_2),
    )
    return (final.reshape(checkpoint.shape), grad.reshape(checkpoint.shape))


def solution(mesh):
    return jax.shard_map(
        shards,
        mesh=mesh,
        in_specs=(
            P(None, None, "lon", "lat"),
            P(None, "lon", "lat"),
            P(None, "lon", "lat"),
            P(None, "lon", "lat"),
            P(None, None, None, "lon", "lat"),
            P(),
            P(None, None, "lon", "lat"),
            P(None, "lon", "lat"),
        ),
        out_specs=(P(None, None, "lon", "lat"), P(None, None, "lon", "lat")),
        check_vma=False,
    )
```
